32 devices in a mesh: grp: 2 (over x), site: 8 (over z, y), sec: 2 (over core).
Axes of the slice: x: 2, y: 2, z: 4, core: 2. Of those that a mesh axis runs over, the one named last changes fastest.
Arguments:
- tensors: bfloat16 [32, 2, 20, 256, 256], P(('grp', 'site'), None, 'sec'), parts along dimension 0, may hold values from -0.25 to 0.25
- sources: int32 [32, 2, 20], P('grp'), parts along dimension 0, may hold values from -1 to 19, as said below
- operators: float32 [2, 2], replicated, may hold values from -1 to 1
- insert_at: int32 [16, 2], P(('grp', 'site')), parts along dimension 0, may hold values from 0 to 1
- schmidt: float32 [32, 20, 256], P('grp', 'sec'), parts along dimension 0, may hold values from 0.2 to 4
Outputs:
- final_env: bfloat16 [16, 2, 20, 256, 256], P(('grp', 'site'), None, 'sec'), parts along dimension 0
- correlation: float32 [32, 2, 2], P(('grp', 'site')), parts along dimension 0
The draws below stay inside these ranges and needn't reach their ends.
There are 2 independent parts, one for each index of `grp`. The reference program is written for one: setup_inputs(seed, part) draws one part's arguments, and reference() takes and returns one part's arrays. A program takes and returns all parts, laid end to end along the dimension named above; an argument that names none is the same for every part. Nothing has to cross between parts.
Inputs may be any that keep to these rules, and one draw needn't show every extreme that they name: Charge conservation: each site i has one charge offset c_i in the finite set (-1, 0, 1), and sources[i, s, r] = r + c_i + 2s - 1 where that lies between 0 and 19, else -1.
All inputs are finite; a program needn't handle non-finite values.
Results may differ from the reference program's by a relative error of at most 0.013.
Values may be sent and summed in bfloat16 or wider, within the bound.
No kernel may reach another device: no remote copies, remote signals or barrier semaphores. Data moves between devices by JAX's collectives and lax.ppermute only.
A program may use at most 128 MiB of HBM per device.

```python
import math
import jax
import jax.numpy as jnp
from jax import lax

SECTORS = 20
BLOCK = 256
INSERTS = 2
SECTIONS = 1
PAIRS = 8
CHAIN = 16


def draw_sources(key, part):
    change = jax.random.randint(key, (CHAIN,), -1, 2, dtype=jnp.int32)
    sector = jnp.arange(SECTORS, dtype=jnp.int32)
    upper = sector[None, :] + change[:, None] - 1
    lower = sector[None, :] + change[:, None] + 1
    both = jnp.stack([upper, lower], axis=1)
    inside = (both >= 0) & (both < SECTORS)
    return jnp.where(inside, both, -1).astype(jnp.int32)


def draw_schmidt(key, part):
    sector = jnp.arange(SECTORS, dtype=jnp.float32) / SECTORS
    base = jnp.exp(jax.random.uniform(key, (CHAIN, SECTORS, BLOCK), jnp.float32, math.log(0.3), 0.0))
    rising = jnp.power(3.0, sector)
    return (base * rising[None, :, None]).astype(jnp.float32)


def touch_ends(result, own_key, low, largest):
    longest = result.shape.index(max(result.shape))
    spots = []
    for shift in (0, 1):
        where = [jax.random.randint(jax.random.fold_in(own_key, axis), (), 0, length) for axis, length in enumerate(result.shape)]
        where[longest] = (where[longest] + shift) % result.shape[longest]
        spots.append(tuple(where))
    return result.at[spots[0]].set(low).at[spots[1]].set(largest)


def block_scale(own_key, dims, split, least, top_value):
    loudness, own = 1.0, jax.random.fold_in(own_key, 6)
    for axis_at, blocks in split:
        heights = jnp.exp(jax.random.uniform(jax.random.fold_in(own, axis_at), (blocks,), jnp.float32, least / len(split), top_value / len(split)))
        loudness = loudness * jnp.repeat(heights, dims[axis_at] // blocks).reshape([-1 if axis == axis_at else 1 for axis in range(len(dims))])
    return loudness


def noise(stream_key, shape, spread, most, cuts=(), kind=jnp.bfloat16):
    values = spread * jax.random.normal(stream_key, shape, jnp.float32)
    if cuts:
        values = values * block_scale(stream_key, shape, cuts, -0.22, 0.18)
    return jnp.clip(values, -most, most).astype(kind)


def setup_inputs(seed: int = 0, part: int = 0) -> dict:
    streams_of = jax.random.split(jax.random.key(seed), 6)
    part_splits = jax.random.split(jax.random.fold_in(streams_of[5], part), 6)
    tensors = noise(part_splits[0], (CHAIN, 2, SECTORS, BLOCK, BLOCK), (2 * BLOCK) ** -0.5, 0.25, ((0, 8), (2, 2)))
    sources = draw_sources(jax.random.fold_in(jax.random.fold_in(streams_of[5], part), 71), part)
    operators = jnp.clip(jax.random.uniform(streams_of[2], (INSERTS, 2), jnp.float32, -1.0, 1.0), -1.0, 1.0)
    insert_at = touch_ends(jax.random.randint(part_splits[3], (PAIRS, INSERTS), 0, 2), jax.random.fold_in(part_splits[3], 1), 0, 1).astype(jnp.int32)
    schmidt = draw_schmidt(jax.random.fold_in(jax.random.fold_in(streams_of[5], part), 71), part)
    return {"tensors": tensors, "sources": sources, "operators": operators, "insert_at": insert_at, "schmidt": schmidt}


def take_blocks(environment, source_rows):
    count = environment.shape[1]
    position = jnp.clip(source_rows, 0, count - 1).astype(jnp.int32)
    picked = jnp.take(environment, position, axis=1)
    return jnp.where((source_rows >= 0)[None, :, :, None, None], picked, jnp.zeros((), environment.dtype))


def advance(environment, blocks, source_rows, weight):
    picked = take_blocks(environment, source_rows)
    middle = jnp.einsum('ksrab,srbc->ksrac', picked.astype(jnp.float32), blocks.astype(jnp.float32)).astype(jnp.bfloat16)
    terms = jnp.einsum('srba,ksrbc->ksrac', blocks.astype(jnp.float32), middle.astype(jnp.float32))
    return jnp.sum(terms * weight[:, :, None, None, None], axis=1).astype(jnp.bfloat16)


def measure(environment, radius):
    diagonal = jnp.diagonal(environment.astype(jnp.float32), axis1=2, axis2=3)
    return jnp.sum(diagonal * (radius * radius)[None], axis=(1, 2))


def reference(tensors, sources, operators, insert_at, schmidt):
    extra = 2 * SECTIONS
    padded_tensors = jnp.concatenate([tensors, jnp.zeros((extra,) + tensors.shape[1:], tensors.dtype)], axis=0)
    padded_sources = jnp.concatenate([sources, jnp.full((extra,) + sources.shape[1:], -1, jnp.int32)], axis=0)
    padded_schmidt = jnp.concatenate([schmidt, jnp.zeros((extra,) + schmidt.shape[1:], jnp.float32)], axis=0)
    unit_weight = jnp.ones_like(operators)

    def one_anchor(anchor):
        def rows(array, section):
            start = (2 * (anchor + section)).astype(jnp.int32)
            return lax.dynamic_slice_in_dim(array, start, 2, 0)

        blocks = rows(padded_tensors, 0)
        source_rows = rows(padded_sources, 0)
        radius_rows = rows(padded_schmidt, 0)
        chosen = lax.dynamic_index_in_dim(insert_at, anchor.astype(jnp.int32), 0, keepdims=False)[:, None]
        first_weight = jnp.where(chosen == 0, operators, jnp.float32(1.0))
        second_weight = jnp.where(chosen == 1, operators, jnp.float32(1.0))
        lead = blocks[0].astype(jnp.float32)
        squares = jnp.einsum('srba,srbc->srac', lead, lead)
        squares = jnp.where((source_rows[0] >= 0)[:, :, None, None], squares, jnp.float32(0.0))
        environment = jnp.sum(first_weight[:, :, None, None, None] * squares[None], axis=1).astype(jnp.bfloat16)
        first_value = measure(environment, radius_rows[0])
        environment = advance(environment, blocks[1], source_rows[1], second_weight)
        section_rows = [jnp.stack([first_value, measure(environment, radius_rows[1])])]
        for section in range(1, SECTIONS + 1):
            blocks = rows(padded_tensors, section)
            source_rows = rows(padded_sources, section)
            radius_rows = rows(padded_schmidt, section)
            measured = []
            for within in range(2):
                environment = advance(environment, blocks[within], source_rows[within], unit_weight)
                measured.append(measure(environment, radius_rows[within]))
            section_rows.append(jnp.stack(measured))
        return jnp.stack(section_rows), environment

    measured_all, ends = lax.map(one_anchor, jnp.arange(PAIRS, dtype=jnp.int32))
    columns = []
    for section in range(SECTIONS + 1):
        column = measured_all[:, section]
        shifted = jnp.concatenate([jnp.zeros((section,) + column.shape[1:], jnp.float32), column[:PAIRS - section]], axis=0)
        columns.append(shifted.reshape(CHAIN, INSERTS))
    correlation = jnp.stack(columns, axis=1)
    final_env = jnp.concatenate([jnp.zeros((SECTIONS,) + ends.shape[1:], jnp.bfloat16), ends[:PAIRS - SECTIONS]], axis=0)
    return final_env, correlation
```

```python
import functools

import jax
import jax.numpy as jnp
from jax import lax
from jax.experimental import pallas as pl
from jax.experimental.pallas import tpu as pltpu
from jax.sharding import PartitionSpec as P

F32 = jnp.float32
BF16 = jnp.bfloat16
HALO = 2
RUNS = ((2, 5), (0, 2), (5, 8), (8, 10))


class Place:
    def __init__(self, sources, width):
        self.core = lax.axis_index("sec")
        self.pair = lax.axis_index("site")
        self.width = width
        middle = sources.shape[2] // 2
        sign = 2 * self.core - 1
        self.steps = []
        for site in range(2):
            charge = sources[2 * self.pair + site, 0, middle] - middle + 1
            self.steps.append([sign * (charge + 2 * state - 1) for state in range(2)])

    def local(self, b):
        return jnp.where(self.core == 0, self.width - 1 - b, b)


def dot(a, b):
    return jnp.dot(a, b, preferred_element_type=F32)


def dot_t(a, b):
    return lax.dot_general(a, b, (((0,), (0,)), ((), ())), preferred_element_type=F32)


def diagonal_row(block):
    half = block.shape[0] // 2
    row = lax.broadcasted_iota(jnp.int32, (half, half), 0)
    col = lax.broadcasted_iota(jnp.int32, (half, half), 1)
    parts = [
        jnp.sum(jnp.where(row == col, block[at : at + half, at : at + half], 0.0), axis=0, keepdims=True)
        for at in (0, half)
    ]
    return jnp.concatenate(parts, axis=1)


def pack(first, second):
    half = first.shape[0] // 2
    row = lax.broadcasted_iota(jnp.int32, (half, half), 0)
    col = lax.broadcasted_iota(jnp.int32, (half, half), 1)
    upper = row <= col

    def mixed(at):
        cut = slice(at, at + half)
        return jnp.where(upper, first[cut, cut], second[cut, cut])

    top = jnp.concatenate([mixed(0), first[:half, half:]], axis=1)
    bottom = jnp.concatenate([second[half:, :half], mixed(half)], axis=1)
    return jnp.concatenate([top, bottom], axis=0).astype(BF16)


def unpack(packed, diagonal, valid):
    half = packed.shape[0] // 2
    packed = jnp.where(valid, packed.astype(F32), 0.0)
    diagonal = jnp.where(valid, diagonal.astype(F32), 0.0)
    turned = packed.T
    row = lax.broadcasted_iota(jnp.int32, (half, half), 0)
    col = lax.broadcasted_iota(jnp.int32, (half, half), 1)

    def low(at):
        cut = slice(at, at + half)
        return jnp.where(row <= col, packed[cut, cut], turned[cut, cut])

    def high(at):
        cut = slice(at, at + half)
        mirrored = jnp.where(row < col, turned[cut, cut], packed[cut, cut])
        return jnp.where(row == col, diagonal[:, cut], mirrored)

    def whole(corner, ne, sw):
        top = jnp.concatenate([corner(0), ne], axis=1)
        bottom = jnp.concatenate([sw, corner(half)], axis=1)
        return jnp.concatenate([top, bottom], axis=0).astype(BF16)

    first = whole(low, packed[:half, half:], turned[half:, :half])
    second = whole(high, turned[:half, half:], packed[half:, :half])
    return first, second


def advance(pair_of, blocks, weight=None):
    size = blocks.shape[-1]
    middles = []
    for state in range(2):
        middle = dot(pair_of(state), blocks[state])
        halves = []
        for insert in range(2):
            part = middle[insert * size : (insert + 1) * size]
            if weight is not None:
                part = part * weight[insert][state]
            halves.append(part.astype(BF16))
        middles.append(jnp.concatenate(halves, axis=1))
    both = dot_t(blocks.reshape(2 * size, size), jnp.concatenate(middles, axis=0))
    return both[:, :size], both[:, size:]


def squares(place, blocks, weight, b):
    terms = [dot_t(blocks[state], blocks[state]) for state in range(2)]
    out = []
    for insert in range(2):
        total = 0.0
        for state in range(2):
            inside = b + place.steps[0][state] < place.width
            total = total + jnp.where(inside, weight[insert][state], 0.0) * terms[state]
        out.append(total)
    return out


def chosen_weights(operators, insert_at, which):
    return [
        [jnp.where(insert_at[0, k] == which, operators[k, s], 1.0) for s in range(2)] for k in range(2)
    ]


def trace_row(block, radius):
    return diagonal_row(block.astype(BF16).astype(F32)) * (radius * radius)


class Loads:
    def __init__(self):
        self.waiting = {}

    def start(self, key, source, target, sem):
        copy = pltpu.make_async_copy(source, target, sem)
        copy.start()
        self.waiting[key] = copy

    def wait(self, *keys):
        for key in keys:
            if key in self.waiting:
                self.waiting.pop(key).wait()


def first_kernel(width, run, sources, operators, insert_at, tensors, schmidt,
                 sent, boundary, traces, t0, t1, env, radius, sems):
    place = Place(sources, width)
    size = tensors.shape[-1]
    lo, hi = run
    count = hi - lo
    base = lo + jnp.minimum(place.steps[1][0], place.steps[1][1])
    loads = Loads()
    loads.start("radius", schmidt.at[pl.ds(2 * place.pair, 2)], radius, sems.at[0])
    needed = [base + i for i in range(count + 2)]
    for i, b in enumerate(needed + [0, 1]):
        loads.start(("t0", i), tensors.at[0, :, place.local(b)], t0.at[i], sems.at[1 + i])
    for i in range(count):
        loads.start(("t1", i), tensors.at[1, :, place.local(lo + i)], t1.at[i], sems.at[1 + count + 4 + i])
    u = chosen_weights(operators, insert_at, 0)
    v = chosen_weights(operators, insert_at, 1)
    traces[...] = jnp.zeros_like(traces)
    for i, b in enumerate(needed + [0, 1]):
        loads.wait(("t0", i))
        parts = squares(place, t0[i], u, b)
        for k in range(2):
            if i < count + 2:
                env[i, k * size : (k + 1) * size] = parts[k].astype(BF16)
            else:
                boundary[i - count - 2, k * size : (k + 1) * size] = parts[k].astype(BF16)
    loads.wait("radius")
    rows = []
    for i in range(count):
        loads.wait(("t1", i))
        parts = advance(lambda s: env[lo + i + place.steps[1][s] - base], t1[i], v)
        store_packed(sent, i, parts, rows)
        for k in range(2):
            row = radius[1, pl.ds(place.local(lo + i), 1)]
            traces[4 + k : 5 + k] += trace_row(parts[k], row)
    store_diagonals(sent, count, rows)


def store_packed(sent, i, parts, rows):
    size = parts[0].shape[0]
    sent[i * size : (i + 1) * size] = pack(*parts)
    rows.append(diagonal_row(parts[1]))


def store_diagonals(sent, count, rows):
    size = rows[0].shape[1]
    pad = jnp.zeros((16 - count, size), F32)
    sent[count * size : count * size + 16] = jnp.concatenate(rows + [pad], axis=0).astype(BF16)


def second_kernel(width, runs, sources, operators, insert_at, tensors, schmidt, halo, old_traces,
                  *rest):
    sents, rest = rest[: len(runs)], rest[len(runs) :]
    traces, t0, t1, env, radius, sems = rest
    place = Place(sources, width)
    size = tensors.shape[-1]
    loads = Loads()
    loads.start("radius", schmidt.at[pl.ds(2 * place.pair, 2)], radius, sems.at[0])
    for b in range(width):
        loads.start(("t0", b), tensors.at[0, :, place.local(b)], t0.at[b], sems.at[1 + b])
    loads.start("halo", halo, env.at[pl.ds(0, 2)], sems.at[1 + 2 * width])
    order = [b for lo, hi in runs for b in range(lo, hi)]
    for b in order:
        loads.start(("t1", b), tensors.at[1, :, place.local(b)], t1.at[b], sems.at[1 + width + b])
    u = chosen_weights(operators, insert_at, 0)
    v = chosen_weights(operators, insert_at, 1)
    env[HALO + width :] = jnp.zeros_like(env[HALO + width :])
    traces[...] = old_traces[...]
    loads.wait("radius")
    for b in range(width):
        loads.wait(("t0", b))
        parts = squares(place, t0[b], u, b)
        row = radius[0, pl.ds(place.local(b), 1)]
        for k in range(2):
            env[HALO + b, k * size : (k + 1) * size] = parts[k].astype(BF16)
            traces[k : k + 1] += trace_row(parts[k], row)
    loads.wait("halo")
    for (lo, hi), sent in zip(runs, sents):
        rows = []
        for b in range(lo, hi):
            loads.wait(("t1", b))
            parts = advance(lambda s: env[HALO + b + place.steps[1][s]], t1[b], v)
            store_packed(sent, b - lo, parts, rows)
            row = radius[1, pl.ds(place.local(b), 1)]
            for k in range(2):
                traces[4 + k : 5 + k] += trace_row(parts[k], row)
        store_diagonals(sent, hi - lo, rows)


def mirrored_halo(b):
    return HALO - 1 - b


def receive_kernel(width, runs, sources, tensors, schmidt, halo, old_traces, *rest):
    arrived, rest = rest[: len(runs)], rest[len(runs) :]
    out, traces, t0, env, radius, sems = rest
    place = Place(sources, width)
    size = tensors.shape[-1]
    valid = place.pair > 0
    loads = Loads()
    loads.start("radius", schmidt.at[pl.ds(2 * place.pair, 2)], radius, sems.at[0])
    for b in range(width):
        loads.start(("t0", b), tensors.at[0, :, place.local(b)], t0.at[b], sems.at[1 + b])
    traces[...] = old_traces[...]
    env[HALO + width :] = jnp.zeros_like(env[HALO + width :])

    def put(buffer, i, count, slot):
        parts = unpack(buffer[i * size : (i + 1) * size], buffer[count * size : count * size + 16][i : i + 1], valid)
        for k in range(2):
            env[slot, k * size : (k + 1) * size] = parts[k]

    for i in range(HALO):
        put(halo, i, HALO, HALO - 1 - i)
    for (lo, hi), buffer in zip(runs, arrived):
        for b in range(lo, hi):
            put(buffer, b - lo, hi - lo, HALO + b)
    loads.wait("radius")
    for b in range(width):
        loads.wait(("t0", b))
        parts = advance(lambda s: env[HALO + b + place.steps[0][s]], t0[b])
        row = radius[0, pl.ds(place.local(b), 1)]
        for k in range(2):
            out[b, k * size : (k + 1) * size] = parts[k].astype(BF16)
            traces[2 + k : 3 + k] += trace_row(parts[k], row)


def last_kernel(width, sources, tensors, schmidt, halo, middle, old_traces, out, traces, t1, env, stage, radius, sems):
    place = Place(sources, width)
    size = tensors.shape[-1]
    loads = Loads()
    loads.start("radius", schmidt.at[pl.ds(2 * place.pair, 2)], radius, sems.at[0])
    for b in range(width):
        loads.start(("t1", b), tensors.at[1, :, place.local(b)], t1.at[b], sems.at[1 + b])
    loads.start("halo", halo, env.at[pl.ds(0, 2)], sems.at[1 + width])
    loads.start("middle", middle, env.at[pl.ds(HALO, width)], sems.at[2 + width])
    traces[...] = old_traces[...]
    env[HALO + width :] = jnp.zeros_like(env[HALO + width :])
    loads.wait("radius", "halo", "middle")
    stores = Loads()
    for b in range(width):
        loads.wait(("t1", b))
        parts = advance(lambda s: env[HALO + b + place.steps[1][s]], t1[b])
        row = radius[1, pl.ds(place.local(b), 1)]
        for k in range(2):
            stage[b, k] = parts[k].astype(BF16)
            traces[6 + k : 7 + k] += trace_row(parts[k], row)
        stores.start(b, stage.at[b], out.at[0, :, place.local(b)], sems.at[3 + width + b])
    for b in range(width):
        stores.wait(b)


SMEM = pl.BlockSpec(memory_space=pltpu.SMEM)
VMEM = pl.BlockSpec(memory_space=pltpu.VMEM)
HBM = pl.BlockSpec(memory_space=pl.ANY)
PARAMS = pltpu.CompilerParams(vmem_limit_bytes=56 * 2**20)


def shards(tensors, sources, operators, insert_at, schmidt):
    width, size = tensors.shape[2], tensors.shape[-1]
    pairs = lax.axis_size("site")
    ring = [(i, (i + 1) % pairs) for i in range(pairs)]
    swap = [(0, 1), (1, 0)]

    def message(run):
        return jax.ShapeDtypeStruct(((run[1] - run[0]) * size + 16, size), BF16)

    trace_shape = jax.ShapeDtypeStruct((8, size), F32)
    edge_shape = jax.ShapeDtypeStruct((HALO, 2 * size, size), BF16)
    tensor_room = lambda n: pltpu.VMEM((n, 2, size, size), BF16)
    env_room = lambda n: pltpu.VMEM((n, 2 * size, size), BF16)
    radius_room = pltpu.VMEM((2,) + schmidt.shape[1:], F32)

    run = RUNS[0]
    count = run[1] - run[0]
    sent0, boundary, traces = pl.pallas_call(
        functools.partial(first_kernel, width, run),
        out_shape=(message(run), edge_shape, trace_shape),
        in_specs=[SMEM, SMEM, SMEM, HBM, HBM],
        out_specs=(VMEM, VMEM, VMEM),
        scratch_shapes=[tensor_room(count + 4), tensor_room(count), env_room(count + 2), radius_room,
                        pltpu.SemaphoreType.DMA((1 + 2 * count + 4,))],
        compiler_params=PARAMS,
    )(sources, operators, insert_at, tensors, schmidt)
    halo = lax.ppermute(boundary, "sec", swap)
    halo = halo[::-1]
    got = [lax.ppermute(sent0, "site", ring)]
    runs = RUNS[1:]
    *sents, traces = pl.pallas_call(
        functools.partial(second_kernel, width, runs),
        out_shape=tuple(message(r) for r in runs) + (trace_shape,),
        in_specs=[SMEM, SMEM, SMEM, HBM, HBM, HBM, VMEM],
        out_specs=(VMEM,) * (len(runs) + 1),
        scratch_shapes=[tensor_room(width), tensor_room(width), env_room(width + 2 * HALO), radius_room,
                        pltpu.SemaphoreType.DMA((2 + 2 * width,))],
        compiler_params=PARAMS,
    )(sources, operators, insert_at, tensors, schmidt, halo, traces)
    got += [lax.ppermute(s, "site", ring) for s in sents]
    halo = lax.ppermute(got[1], "sec", swap)
    middle, traces = pl.pallas_call(
        functools.partial(receive_kernel, width, RUNS),
        out_shape=(jax.ShapeDtypeStruct((width, 2 * size, size), BF16), trace_shape),
        in_specs=[SMEM, HBM, HBM, VMEM, VMEM] + [VMEM] * len(RUNS),
        out_specs=(VMEM, VMEM),
        scratch_shapes=[tensor_room(width), env_room(width + 2 * HALO), radius_room,
                        pltpu.SemaphoreType.DMA((1 + width,))],
        compiler_params=PARAMS,
    )(sources, tensors, schmidt, halo, traces, *got)
    halo = lax.ppermute(middle[:HALO], "sec", swap)[::-1]
    final, traces = pl.pallas_call(
        functools.partial(last_kernel, width),
        out_shape=(jax.ShapeDtypeStruct((1, 2, width, size, size), BF16), trace_shape),
        in_specs=[SMEM, HBM, HBM, HBM, HBM, VMEM],
        out_specs=(HBM, VMEM),
        scratch_shapes=[tensor_room(width), env_room(width + 2 * HALO), pltpu.VMEM((width, 2, size, size), BF16),
                        radius_room, pltpu.SemaphoreType.DMA((3 + 2 * width,))],
        compiler_params=PARAMS,
    )(sources, tensors, schmidt, halo, middle, traces)
    other = lax.ppermute(traces, "sec", swap)
    correlation = jnp.sum(traces + other, axis=1).reshape(2, 2, 2)
    return final, correlation


def solution(mesh):
    placed = (
        P(("grp", "site"), None, "sec", None, None),
        P("grp", None, None),
        P(),
        P(("grp", "site"), None),
        P("grp", "sec", None),
    )
    return jax.shard_map(
        shards,
        mesh=mesh,
        in_specs=placed,
        out_specs=(P(("grp", "site"), None, "sec", None, None), P(("grp", "site"), None, None)),
        check_vma=False,
    )
```

```python
import functools

import jax
import jax.numpy as jnp
from jax import lax
from jax.experimental import pallas as pl
from jax.experimental.pallas import tpu as pltpu
from jax.sharding import PartitionSpec as P

F32 = jnp.float32
BF16 = jnp.bfloat16
REACH = 4
HALO = 2
class Place:
    def __init__(self, sources, width):
        self.core = lax.axis_index("sec")
        self.pair = lax.axis_index("site")
        self.width = width
        middle = sources.shape[2] // 2
        sign = 2 * self.core - 1
        self.steps = []
        for site in range(2):
            charge = sources[2 * self.pair + site, 0, middle] - middle + 1
            self.steps.append([sign * (charge + 2 * state - 1) for state in range(2)])

    def local(self, b):
        return jnp.where(self.core == 0, self.width - 1 - b, b)


def dot(a, b):
    return jnp.dot(a, b, preferred_element_type=F32)


def dot_t(a, b):
    return lax.dot_general(a, b, (((0,), (0,)), ((), ())), preferred_element_type=F32)


def diagonal_row(block):
    half = block.shape[0] // 2
    row = lax.broadcasted_iota(jnp.int32, (half, half), 0)
    col = lax.broadcasted_iota(jnp.int32, (half, half), 1)
    parts = [
        jnp.sum(jnp.where(row == col, block[at : at + half, at : at + half], 0.0), axis=0, keepdims=True)
        for at in (0, half)
    ]
    return jnp.concatenate(parts, axis=1)


def pack(first, second):
    half = first.shape[0] // 2
    row = lax.broadcasted_iota(jnp.int32, (half, half), 0)
    col = lax.broadcasted_iota(jnp.int32, (half, half), 1)
    upper = row <= col

    def mixed(at):
        cut = slice(at, at + half)
        return jnp.where(upper, first[cut, cut], second[cut, cut])

    top = jnp.concatenate([mixed(0), first[:half, half:]], axis=1)
    bottom = jnp.concatenate([second[half:, :half], mixed(half)], axis=1)
    return jnp.concatenate([top, bottom], axis=0).astype(BF16)


def unpack(packed, diagonal, valid):
    half = packed.shape[0] // 2
    packed = jnp.where(valid, packed, jnp.zeros_like(packed))
    diagonal = jnp.where(valid, diagonal.astype(F32), 0.0)
    turned = packed.T
    row = lax.broadcasted_iota(jnp.int32, (half, half), 0)
    col = lax.broadcasted_iota(jnp.int32, (half, half), 1)

    def corners(at):
        cut = slice(at, at + half)
        straight, mirrored = packed[cut, cut].astype(F32), turned[cut, cut].astype(F32)
        low = jnp.where(row <= col, straight, mirrored)
        high = jnp.where(row == col, diagonal[:, cut], jnp.where(row < col, mirrored, straight))
        return low.astype(BF16), high.astype(BF16)

    def whole(north, ne, sw, south):
        top = jnp.concatenate([north, ne], axis=1)
        bottom = jnp.concatenate([sw, south], axis=1)
        return jnp.concatenate([top, bottom], axis=0)

    north, south = corners(0), corners(half)
    first = whole(north[0], packed[:half, half:], turned[half:, :half], south[0])
    second = whole(north[1], turned[:half, half:], packed[half:, :half], south[1])
    return first, second


def advance(env, slots, blocks, weight=None):
    size = blocks.shape[-1]
    middles = []
    for state in range(2):
        turned = blocks[state].T
        halves = []
        for insert in range(2):
            part = dot(turned, env[slots[state], insert * size : (insert + 1) * size])
            if weight is not None:
                part = part * weight[insert][state]
            halves.append(part.astype(BF16))
        middles.append(jnp.concatenate(halves, axis=0))
    both = dot(jnp.concatenate(middles, axis=1), blocks.reshape(2 * size, size))
    return both[:size], both[size:]


def squares(place, blocks, weight, b):
    terms = [dot(blocks[state].T, blocks[state]) for state in range(2)]
    out = []
    for insert in range(2):
        total = 0.0
        for state in range(2):
            inside = b + place.steps[0][state] < place.width
            total = total + jnp.where(inside, weight[insert][state], 0.0) * terms[state]
        out.append(total)
    return out


def chosen_weights(operators, insert_at, which):
    return [
        [jnp.where(insert_at[0, k] == which, operators[k, s], 1.0) for s in range(2)] for k in range(2)
    ]


def add_traces(place, traces, at, site, b, parts, radius):
    row = radius[place.local(b), pl.ds(2 * place.pair + site, 1)]
    for k in range(2):
        traces[at + k : at + k + 1] += diagonal_row(parts[k].astype(BF16).astype(F32)) * (row * row)


def slots_of(place, site, b):
    return [REACH + b + place.steps[site][state] for state in range(2)]


def store_env(env, slot, parts):
    size = parts[0].shape[0]
    for k in range(2):
        env[slot, k * size : (k + 1) * size] = parts[k].astype(BF16)


def send(place, env, t1, weight, traces, radius, sent, run):
    rows = []
    lo, hi = run
    for b in range(lo, hi):
        parts = advance(env, slots_of(place, 1, b), t1[b], weight)
        size = parts[0].shape[0]
        sent[(b - lo) * size : (b - lo + 1) * size] = pack(*parts)
        rows.append(diagonal_row(parts[1]))
        add_traces(place, traces, 4, 1, b, parts, radius)
    rows.append(jnp.zeros((16 - len(rows), size), F32))
    sent[(hi - lo) * size : (hi - lo) * size + 16] = jnp.concatenate(rows, axis=0).astype(BF16)


def take(place, buffer, i, count, env, slot):
    size = buffer.shape[1]
    diagonal = buffer[count * size : count * size + 16][i : i + 1]
    store_env(env, slot, unpack(buffer[i * size : (i + 1) * size], diagonal, place.pair > 0))


class Loads:
    def __init__(self):
        self.waiting = {}

    def start(self, key, source, target, sem):
        copy = pltpu.make_async_copy(source, target, sem)
        copy.start()
        self.waiting[key] = copy

    def wait(self, *keys):
        for key in keys:
            if key in self.waiting:
                self.waiting.pop(key).wait()


def first_kernel(width, run, sources, operators, insert_at, tensors, schmidt,
                 sent, edge, env, t0, t1, radius, traces, sems):
    place = Place(sources, width)
    lo, hi = run
    loads = Loads()
    ends = list(range(lo, width)) + list(range(lo))
    near = [b for b in ends if lo - HALO <= b < hi + HALO]
    for b in near:
        loads.start(("t0", b), tensors.at[0, :, place.local(b)], t0.at[b], sems.at[0, b])
    for b in range(lo, hi):
        loads.start(("t1", b), tensors.at[1, :, place.local(b)], t1.at[b], sems.at[1, b])
    loads.start("radius", schmidt, radius, sems.at[0, width])
    for b in ends:
        if b not in near:
            loads.start(("t0", b), tensors.at[0, :, place.local(b)], t0.at[b], sems.at[0, b])
    for b in ends:
        if not lo <= b < hi:
            loads.start(("t1", b), tensors.at[1, :, place.local(b)], t1.at[b], sems.at[1, b])
    u = chosen_weights(operators, insert_at, 0)
    v = chosen_weights(operators, insert_at, 1)
    traces[...] = jnp.zeros_like(traces)
    env[REACH + width :] = jnp.zeros_like(env[REACH + width :])
    for b in near:
        loads.wait(("t0", b))
        parts = squares(place, t0[b], u, b)
        store_env(env, REACH + b, parts)
        if b < HALO:
            store_env(edge, HALO - 1 - b, parts)
            edge[2 * HALO - 1 - b] = t0[b].reshape(edge.shape[1:])
    for b in range(lo, hi):
        loads.wait(("t1", b))
    loads.wait("radius")
    send(place, env, t1, v, traces, radius, sent, run)
    for b in ends:
        loads.wait(("t0", b), ("t1", b))


def second_kernel(width, first_run, runs, sources, operators, insert_at, old_env, halo, t0, t1, radius, old_traces, *rest):
    env, sents, traces = rest[0], rest[1:-1], rest[-1]
    place = Place(sources, width)
    size = t0.shape[-1]
    u = chosen_weights(operators, insert_at, 0)
    v = chosen_weights(operators, insert_at, 1)
    traces[...] = old_traces[...]
    for i in range(HALO):
        env[REACH - HALO + i] = halo[i]
    lo, hi = first_run
    for b in range(width):
        if not lo - HALO <= b < hi + HALO:
            parts = squares(place, t0[b], u, b)
            store_env(env, REACH + b, parts)
        else:
            parts = [env[REACH + b, k * size : (k + 1) * size] for k in range(2)]
        add_traces(place, traces, 0, 0, b, parts, radius)
    for run, sent in zip(runs, sents):
        send(place, env, t1, v, traces, radius, sent, run)


def open_kernel(width, run, sources, buffer, env, piece):
    place = Place(sources, width)
    env[REACH + width :] = jnp.zeros_like(env[REACH + width :])
    lo, hi = run
    size = buffer.shape[1]
    for b in range(lo, hi):
        take(place, buffer, b - lo, hi - lo, env, REACH + b)
    piece[: HALO * size] = buffer[: HALO * size]
    piece[HALO * size :] = buffer[(hi - lo) * size :]


def middle_blocks(place, todo, env, middle, t0, traces, radius):
    for b in range(*todo):
        parts = advance(env, slots_of(place, 0, b), t0[b])
        store_env(middle, REACH + b, parts)
        add_traces(place, traces, 2, 0, b, parts, radius)


def final_blocks(place, todo, middle, t1, traces, radius, stage, out, sems):
    stores = Loads()
    for b in range(*todo):
        parts = advance(middle, slots_of(place, 1, b), t1[b])
        for k in range(2):
            stage[b, k] = parts[k].astype(BF16)
        stores.start(b, stage.at[b], out.at[0, :, place.local(b)], sems.at[b])
        add_traces(place, traces, 6, 1, b, parts, radius)
    return stores


def edge_kernel(width, known, sources, t0, t1, halo, radius, old_traces, old_env, ours, *rest):
    beyond, (out, env, middle, traces, stage, sems) = rest[:2], rest[2:]
    place = Place(sources, width)
    traces[...] = old_traces[...]
    middle[REACH + width :] = jnp.zeros_like(middle[REACH + width :])
    for i in range(HALO):
        take(place, ours, i, HALO, env, REACH + i)
        for j in range(2):
            take(place, beyond[j], i, HALO, env, REACH - 1 - i - HALO * j)
    for i in range(HALO):
        blocks = halo[HALO + i].reshape(t0.shape[1:])
        store_env(middle, REACH - HALO + i, advance(env, slots_of(place, 0, i - HALO), blocks))
    middle_blocks(place, (0, known - HALO), env, middle, t0, traces, radius)
    last = (0, known - 2 * HALO)
    final_blocks(place, last, middle, t1, traces, radius, stage, out, sems).wait(*range(*last))


def next_kernel(width, run, sources, t0, t1, radius, old_traces, buffer, old_env, old_middle, old_out,
                out, env, middle, traces, *rest):
    totals, (stage, sems) = rest[:-2], rest[-2:]
    place = Place(sources, width)
    lo, hi = run
    upto = (width, width) if hi == width else (hi - HALO, hi - 2 * HALO)
    for b in range(lo, hi):
        take(place, buffer, b - lo, hi - lo, env, REACH + b)
    traces[...] = old_traces[...]
    middle_blocks(place, (lo - HALO, upto[0]), env, middle, t0, traces, radius)
    last = (lo - 2 * HALO, upto[1])
    stores = final_blocks(place, last, middle, t1, traces, radius, stage, out, sems)
    for total in totals:
        sums = jnp.sum(traces[...], axis=1, keepdims=True)
        for j in range(2):
            for t in range(2):
                at = 4 * j + 2 * t
                total[j, t : t + 1] = jnp.concatenate([sums[at : at + 1], sums[at + 1 : at + 2]], axis=1)
    stores.wait(*range(*last))


SMEM = pl.BlockSpec(memory_space=pltpu.SMEM)
VMEM = pl.BlockSpec(memory_space=pltpu.VMEM)
HBM = pl.BlockSpec(memory_space=pl.ANY)
PARAMS = pltpu.CompilerParams(vmem_limit_bytes=28 * 2**20)
RUNS = ((2, 6), (0, 2), (6, 10))


def held(array, near):
    return pltpu.with_memory_space_constraint(array, pltpu.VMEM if near else pltpu.HBM)


def call(kernel, name, scalars, arrays, outs, scratch=(), aliases=None):
    return pl.pallas_call(
        kernel,
        out_shape=tuple((pltpu.VMEM if near else pltpu.HBM)(s, d) for s, d, near in outs),
        in_specs=[SMEM] * len(scalars) + [VMEM if near else HBM for _, near in arrays],
        out_specs=tuple(VMEM if near else HBM for _, _, near in outs),
        scratch_shapes=list(scratch),
        compiler_params=PARAMS,
        input_output_aliases={} if aliases is None else aliases,
        name=name,
    )(*[held(a, False) for a in scalars], *[held(a, near) for a, near in arrays])


def shards(tensors, sources, operators, insert_at, schmidt):
    width, size = tensors.shape[2], tensors.shape[-1]
    pairs = lax.axis_size("site")
    ring = [(i, (i + 1) % pairs) for i in range(pairs)]
    swap = [(0, 1), (1, 0)]
    schmidt = jnp.swapaxes(schmidt, 0, 1)

    def message(run):
        return ((run[1] - run[0]) * size + 16, size), BF16, True

    trace_shape = ((8, size), F32, True)
    env_shape = ((width + REACH + HALO, 2 * size, size), BF16, True)
    tensor_shape = ((width, 2, size, size), BF16, True)
    radius_shape = (schmidt.shape, F32, True)
    out_shape = ((1, 2, width, size, size), BF16, False)
    stage = [pltpu.VMEM((width, 2, size, size), BF16), pltpu.SemaphoreType.DMA((width,))]

    def across(array):
        return lax.ppermute(array, "sec", swap)

    sent, edge, env, t0, t1, radius, traces = call(
        functools.partial(first_kernel, width, RUNS[0]),
        "anchor",
        (sources, operators, insert_at),
        ((tensors, False), (schmidt, False)),
        (
            message(RUNS[0]),
            ((2 * HALO, 2 * size, size), BF16, True),
            env_shape,
            tensor_shape,
            tensor_shape,
            radius_shape,
            trace_shape,
        ),
        [pltpu.SemaphoreType.DMA((2, width + 1))],
    )
    halo = across(edge)
    got = [lax.ppermute(sent, "site", ring)]
    env, *sents, traces = call(
        functools.partial(second_kernel, width, RUNS[0], RUNS[1:]),
        "anchor_rest",
        (sources, operators, insert_at),
        ((env, True), (halo, True), (t0, True), (t1, True), (radius, True), (traces, True)),
        (env_shape,) + tuple(message(r) for r in RUNS[1:]) + (trace_shape,),
        aliases={3: 0},
    )
    got += [lax.ppermute(s, "site", ring) for s in sents]
    env, piece = call(
        functools.partial(open_kernel, width, RUNS[0]),
        "first_run",
        (sources,),
        ((got[0], True),),
        (env_shape, message(RUNS[1])),
    )
    ours, env = lax.optimization_barrier((got[1], env))
    final, env, middle, traces = call(
        functools.partial(edge_kernel, width, RUNS[0][1]),
        "edge",
        (sources,),
        tuple((a, True) for a in (t0, t1, halo, radius, traces, env, ours, across(ours), across(piece))),
        (out_shape, env_shape, env_shape, trace_shape),
        stage,
        {6: 1},
    )
    for run, buffer in zip(RUNS[2:], got[2:]):
        outs = (out_shape, env_shape, env_shape, trace_shape)
        if run[1] == width:
            outs += (((2, 2, 2), F32, True),)
        final, env, middle, traces, *totals = call(
            functools.partial(next_kernel, width, run),
            "run_%d" % run[0],
            (sources,),
            tuple((a, True) for a in (t0, t1, radius, traces, buffer, env, middle)) + ((final, False),),
            outs,
            stage,
            {6: 1, 7: 2, 8: 0},
        )
    return final, totals[0] + across(totals[0])


def solution(mesh):
    placed = (
        P(("grp", "site"), None, "sec", None, None),
        P("grp", None, None),
        P(),
        P(("grp", "site"), None),
        P("grp", "sec", None),
    )
    return jax.shard_map(
        shards,
        mesh=mesh,
        in_specs=placed,
        out_specs=(P(("grp", "site"), None, "sec", None, None), P(("grp", "site"), None, None)),
        check_vma=False,
    )
```

```python
import functools

import jax
import jax.numpy as jnp
from jax import lax
from jax.experimental import pallas as pl
from jax.experimental.pallas import tpu as pltpu
from jax.sharding import PartitionSpec as P

F32 = jnp.float32
BF16 = jnp.bfloat16
REACH = 4
HALO = 2
class Place:
    def __init__(self, width, steps):
        self.core = lax.axis_index("sec")
        self.pair = lax.axis_index("site")
        self.width = width
        self.steps = steps

    def local(self, b):
        return jnp.where(self.core == 0, self.width - 1 - b, b)


def dot(a, b):
    return jnp.dot(a, b, preferred_element_type=F32)


def dot_t(a, b):
    return lax.dot_general(a, b, (((0,), (0,)), ((), ())), preferred_element_type=F32)


def diagonal_row(block):
    half = block.shape[0] // 2
    row = lax.broadcasted_iota(jnp.int32, (half, half), 0)
    col = lax.broadcasted_iota(jnp.int32, (half, half), 1)
    parts = [
        jnp.sum(jnp.where(row == col, block[at : at + half, at : at + half], 0.0), axis=0, keepdims=True)
        for at in (0, half)
    ]
    return jnp.concatenate(parts, axis=1)


def pack(first, second):
    half = first.shape[0] // 2
    row = lax.broadcasted_iota(jnp.int32, (half, half), 0)
    col = lax.broadcasted_iota(jnp.int32, (half, half), 1)
    upper = row <= col

    def mixed(at):
        cut = slice(at, at + half)
        return jnp.where(upper, first[cut, cut], second[cut, cut])

    top = jnp.concatenate([mixed(0), first[:half, half:]], axis=1)
    bottom = jnp.concatenate([second[half:, :half], mixed(half)], axis=1)
    return jnp.concatenate([top, bottom], axis=0).astype(BF16)


def unpack(packed, diagonal, valid):
    half = packed.shape[0] // 2
    packed = jnp.where(valid, packed, jnp.zeros_like(packed))
    diagonal = jnp.where(valid, diagonal.astype(F32), 0.0)
    turned = packed.T
    row = lax.broadcasted_iota(jnp.int32, (half, half), 0)
    col = lax.broadcasted_iota(jnp.int32, (half, half), 1)

    def corners(at):
        cut = slice(at, at + half)
        straight, mirrored = packed[cut, cut].astype(F32), turned[cut, cut].astype(F32)
        low = jnp.where(row <= col, straight, mirrored)
        high = jnp.where(row == col, diagonal[:, cut], jnp.where(row < col, mirrored, straight))
        return low.astype(BF16), high.astype(BF16)

    def whole(north, ne, sw, south):
        top = jnp.concatenate([north, ne], axis=1)
        bottom = jnp.concatenate([sw, south], axis=1)
        return jnp.concatenate([top, bottom], axis=0)

    north, south = corners(0), corners(half)
    first = whole(north[0], packed[:half, half:], turned[half:, :half], south[0])
    second = whole(north[1], turned[:half, half:], packed[half:, :half], south[1])
    return first, second


def advance(env, slots, blocks, weight=None):
    size = blocks.shape[-1]
    middles = []
    for state in range(2):
        turned = blocks[state].T
        halves = []
        for insert in range(2):
            part = dot(turned, env[slots[state], insert * size : (insert + 1) * size])
            if weight is not None:
                part = part * weight[insert][state]
            halves.append(part.astype(BF16))
        middles.append(jnp.concatenate(halves, axis=0))
    both = dot(jnp.concatenate(middles, axis=1), blocks.reshape(2 * size, size))
    return both[:size], both[size:]


def squares(place, blocks, weight, b):
    terms = [dot(blocks[state].T, blocks[state]) for state in range(2)]
    out = []
    for insert in range(2):
        total = 0.0
        for state in range(2):
            inside = b + place.steps[state] < place.width
            total = total + jnp.where(inside, weight[insert][state], 0.0) * terms[state]
        out.append(total)
    return out


def fill_steps(place, sources, steps):
    middle = sources.shape[2] // 2
    for site in range(2):
        charge = sources[2 * place.pair + site, 0, middle] - middle + 1
        for state in range(2):
            steps[2 * site + state] = (2 * place.core - 1) * (charge + 2 * state - 1)


def fill_weights(operators, insert_at, weights):
    for which in range(2):
        for k in range(2):
            for s in range(2):
                weights[which, 2 * k + s] = jnp.where(insert_at[0, k] == which, operators[k, s], 1.0)


def weights_at(weights, which):
    return [[weights[which, 2 * k + s] for s in range(2)] for k in range(2)]


def add_traces(place, traces, at, site, b, parts, radius):
    row = radius[place.local(b), pl.ds(2 * place.pair + site, 1)]
    for k in range(2):
        traces[at + k : at + k + 1] += diagonal_row(parts[k].astype(BF16).astype(F32)) * (row * row)


def slots_of(place, site, b):
    return [REACH + b + place.steps[2 * site + state] for state in range(2)]


def store_env(env, slot, parts):
    size = parts[0].shape[0]
    for k in range(2):
        env[slot, k * size : (k + 1) * size] = parts[k].astype(BF16)


def send_one(place, env, t1, weight, traces, radius, sent, lo, b):
    parts = advance(env, slots_of(place, 1, b), t1[b], weight)
    size = parts[0].shape[0]
    sent[(b - lo) * size : (b - lo + 1) * size] = pack(*parts)
    add_traces(place, traces, 4, 1, b, parts, radius)
    return diagonal_row(parts[1])


def send_rows(sent, rows):
    count, size = len(rows), rows[0].shape[1]
    rows = rows + [jnp.zeros((16 - count, size), F32)]
    sent[count * size : count * size + 16] = jnp.concatenate(rows, axis=0).astype(BF16)


def send(place, env, t1, weight, traces, radius, sent, run):
    send_rows(sent, [send_one(place, env, t1, weight, traces, radius, sent, run[0], b) for b in range(*run)])


def take(place, buffer, i, count, env, slot):
    size = buffer.shape[1]
    diagonal = buffer[count * size : count * size + 16][i : i + 1]
    store_env(env, slot, unpack(buffer[i * size : (i + 1) * size], diagonal, place.pair > 0))


class Loads:
    def __init__(self):
        self.waiting = {}

    def start(self, key, source, target, sem):
        copy = pltpu.make_async_copy(source, target, sem)
        copy.start()
        self.waiting[key] = copy

    def wait(self, *keys):
        for key in keys:
            if key in self.waiting:
                self.waiting.pop(key).wait()


def first_kernel(width, run, sources, operators, insert_at, tensors, schmidt,
                 sent, edge, env, t0, t1, radius, traces, steps, weights, sources_here, operators_here, inserts_here, sems):
    place = Place(width, steps)
    lo, hi = run
    loads = Loads()
    loads.start("sources", sources, sources_here, sems.at[1, 0])
    loads.start("operators", operators, operators_here, sems.at[1, 1])
    loads.start("insert_at", insert_at, inserts_here, sems.at[1, width])
    near = list(range(hi + HALO))
    for b in near:
        loads.start(("t0", b), tensors.at[0, :, place.local(b)], t0.at[b], sems.at[0, b])
    for b in range(lo, hi):
        loads.start(("t1", b), tensors.at[1, :, place.local(b)], t1.at[b], sems.at[1, b])
    loads.start("radius", schmidt, radius, sems.at[0, width])
    traces[...] = jnp.zeros_like(traces)
    env[REACH + width :] = jnp.zeros_like(env[REACH + width :])
    loads.wait("sources", "operators", "insert_at")
    fill_steps(place, sources_here, steps)
    fill_weights(operators_here, inserts_here, weights)
    u, v = weights_at(weights, 0), weights_at(weights, 1)
    for group in [near]:
        for b in group:
            loads.wait(("t0", b))
        for b in group:
            parts = squares(place, t0[b], u, b)
            store_env(env, REACH + b, parts)
            if b < HALO:
                store_env(edge, HALO - 1 - b, parts)
                edge[2 * HALO - 1 - b] = t0[b].reshape(edge.shape[1:])
    for b in range(lo, hi):
        loads.wait(("t1", b))
    loads.wait("radius")
    send(place, env, t1, v, traces, radius, sent, run)


def second_kernel(width, first_run, runs, steps, weights, tensors, old_env, halo, old_t0, old_t1, radius,
                  old_traces, *rest):
    env, t0, t1, sents, (traces, sems) = *rest[:3], rest[3:-2], rest[-2:]
    place = Place(width, steps)
    size = t0.shape[-1]
    lo, hi = first_run
    late = [b for b in range(width) if not lo - HALO <= b < hi + HALO]
    order = [b for run in runs for b in range(*run)]
    loads = Loads()
    for b in late:
        loads.start(("t0", b), tensors.at[0, :, place.local(b)], t0.at[b], sems.at[0, b])
    for b in order:
        loads.start(("t1", b), tensors.at[1, :, place.local(b)], t1.at[b], sems.at[1, b])
    u, v = weights_at(weights, 0), weights_at(weights, 1)
    traces[...] = old_traces[...]
    for i in range(HALO):
        env[REACH - HALO + i] = halo[i]
    for b in range(width):
        if b in late:
            loads.wait(("t0", b))
            parts = squares(place, t0[b], u, b)
            store_env(env, REACH + b, parts)
        else:
            parts = [env[REACH + b, k * size : (k + 1) * size] for k in range(2)]
        add_traces(place, traces, 0, 0, b, parts, radius)
    for b in order:
        loads.wait(("t1", b))
    for run, sent in zip(runs, sents):
        send(place, env, t1, v, traces, radius, sent, run)


def open_kernel(width, runs, steps, *rest):
    buffers, (env, piece) = rest[: len(runs)], rest[len(runs) :]
    place = Place(width, steps)
    env[REACH + width :] = jnp.zeros_like(env[REACH + width :])
    for (lo, hi), buffer in zip(runs, buffers):
        for b in range(lo, hi):
            take(place, buffer, b - lo, hi - lo, env, REACH + b)
    size = buffers[0].shape[1]
    piece[: HALO * size] = buffers[0][: HALO * size]
    piece[HALO * size :] = buffers[0][(runs[0][1] - runs[0][0]) * size :]


def middle_blocks(place, todo, env, middle, t0, traces, radius):
    for b in range(*todo):
        parts = advance(env, slots_of(place, 0, b), t0[b])
        store_env(middle, REACH + b, parts)
        add_traces(place, traces, 2, 0, b, parts, radius)


def final_blocks(place, todo, middle, t1, traces, radius, stage, out, sems):
    stores = Loads()
    for b in range(*todo):
        parts = advance(middle, slots_of(place, 1, b), t1[b])
        for k in range(2):
            stage[b, k] = parts[k].astype(BF16)
        stores.start(b, stage.at[b], out.at[0, :, place.local(b)], sems.at[b])
        add_traces(place, traces, 6, 1, b, parts, radius)
    return stores


def edge_kernel(width, known, steps, t0, t1, halo, radius, old_traces, old_env, ours, *rest):
    beyond, (out, env, middle, traces, stage, sems) = rest[:2], rest[2:]
    place = Place(width, steps)
    traces[...] = old_traces[...]
    middle[REACH + width :] = jnp.zeros_like(middle[REACH + width :])
    for i in range(HALO):
        take(place, ours, i, HALO, env, REACH + i)
        for j in range(2):
            take(place, beyond[j], i, HALO, env, REACH - 1 - i - HALO * j)
    for i in range(HALO):
        blocks = halo[HALO + i].reshape(t0.shape[1:])
        store_env(middle, REACH - HALO + i, advance(env, slots_of(place, 0, i - HALO), blocks))
    middle_blocks(place, (0, known - HALO), env, middle, t0, traces, radius)
    last = (0, known - 2 * HALO)
    final_blocks(place, last, middle, t1, traces, radius, stage, out, sems).wait(*range(*last))


def next_kernel(width, run, steps, t0, t1, radius, old_traces, buffer, old_env, old_middle, old_out,
                out, env, middle, traces, *rest):
    totals, (stage, sems) = rest[:-2], rest[-2:]
    place = Place(width, steps)
    lo, hi = run
    upto = (width, width) if hi == width else (hi - HALO, hi - 2 * HALO)
    for b in range(lo, hi):
        take(place, buffer, b - lo, hi - lo, env, REACH + b)
    traces[...] = old_traces[...]
    middle_blocks(place, (lo - HALO, upto[0]), env, middle, t0, traces, radius)
    last = (lo - 2 * HALO, upto[1])
    stores = final_blocks(place, last, middle, t1, traces, radius, stage, out, sems)
    for total in totals:
        sums = jnp.sum(traces[...], axis=1, keepdims=True)
        for j in range(2):
            for t in range(2):
                at = 4 * j + 2 * t
                total[j, t : t + 1] = jnp.concatenate([sums[at : at + 1], sums[at + 1 : at + 2]], axis=1)
    stores.wait(*range(*last))


SMEM = pl.BlockSpec(memory_space=pltpu.SMEM)
VMEM = pl.BlockSpec(memory_space=pltpu.VMEM)
HBM = pl.BlockSpec(memory_space=pl.ANY)
PARAMS = pltpu.CompilerParams(vmem_limit_bytes=28 * 2**20)
RUNS = ((2, 5), (5, 7), (0, 2), (7, 10))
OPENED = 2


def call(kernel, name, scalars, arrays, outs, scratch=(), aliases=None):
    specs = {pltpu.VMEM: VMEM, pltpu.SMEM: SMEM, pltpu.HBM: HBM}
    where = [pltpu.SMEM] * len(scalars) + [pltpu.VMEM if near else pltpu.HBM for _, near in arrays]
    values = [*scalars, *[a for a, _ in arrays]]
    return pl.pallas_call(
        kernel,
        out_shape=tuple(memory(s, d) for s, d, memory in outs),
        in_specs=[specs[w] for w in where],
        out_specs=tuple(specs[memory] for _, _, memory in outs),
        scratch_shapes=list(scratch),
        compiler_params=PARAMS,
        input_output_aliases={} if aliases is None else aliases,
        name=name,
    )(*[pltpu.with_memory_space_constraint(a, w) for a, w in zip(values, where)])


def shards(tensors, sources, operators, insert_at, schmidt):
    width, size = tensors.shape[2], tensors.shape[-1]
    pairs = lax.axis_size("site")
    ring = [(i, (i + 1) % pairs) for i in range(pairs)]
    swap = [(0, 1), (1, 0)]
    schmidt = jnp.swapaxes(schmidt, 0, 1)

    def message(run):
        return ((run[1] - run[0]) * size + 16, size), BF16, pltpu.VMEM

    trace_shape = ((8, size), F32, pltpu.VMEM)
    env_shape = ((width + REACH + HALO, 2 * size, size), BF16, pltpu.VMEM)
    tensor_shape = ((width, 2, size, size), BF16, pltpu.VMEM)
    radius_shape = (schmidt.shape, F32, pltpu.VMEM)
    out_shape = ((1, 2, width, size, size), BF16, pltpu.HBM)
    stage = [pltpu.VMEM((width, 2, size, size), BF16), pltpu.SemaphoreType.DMA((width,))]

    def across(array):
        return lax.ppermute(array, "sec", swap)

    sent, edge, env, t0, t1, radius, traces, steps, weights = call(
        functools.partial(first_kernel, width, RUNS[0]),
        "anchor",
        (),
        tuple((a, False) for a in (sources, operators, insert_at, tensors, schmidt)),
        (
            message(RUNS[0]),
            ((2 * HALO, 2 * size, size), BF16, pltpu.VMEM),
            env_shape,
            tensor_shape,
            tensor_shape,
            radius_shape,
            trace_shape,
            ((4,), jnp.int32, pltpu.SMEM),
            ((2, 4), F32, pltpu.SMEM),
        ),
        [pltpu.SMEM(a.shape, a.dtype) for a in (sources, operators, insert_at)] + [pltpu.SemaphoreType.DMA((2, width + 1))],
    )
    halo = across(edge)
    got = [lax.ppermute(sent, "site", ring)]
    env, t0, t1, *sents, traces = call(
        functools.partial(second_kernel, width, RUNS[0], RUNS[1:]),
        "anchor_rest",
        (steps, weights),
        ((tensors, False),) + tuple((a, True) for a in (env, halo, t0, t1, radius, traces)),
        (env_shape, tensor_shape, tensor_shape) + tuple(message(r) for r in RUNS[1:]) + (trace_shape,),
        [pltpu.SemaphoreType.DMA((2, width))],
        {3: 0, 5: 1, 6: 2},
    )
    got += [lax.ppermute(s, "site", ring) for s in sents]
    env, piece = call(
        functools.partial(open_kernel, width, RUNS[:OPENED]),
        "first_runs",
        (steps,),
        tuple((a, True) for a in got[:OPENED]),
        (env_shape, message(RUNS[OPENED])),
    )
    ours, env = lax.optimization_barrier((got[OPENED], env))
    final, env, middle, traces = call(
        functools.partial(edge_kernel, width, RUNS[OPENED - 1][1]),
        "edge",
        (steps,),
        tuple((a, True) for a in (t0, t1, halo, radius, traces, env, ours, across(ours), across(piece))),
        (out_shape, env_shape, env_shape, trace_shape),
        stage,
        {6: 1},
    )
    for run, buffer in zip(RUNS[OPENED + 1 :], got[OPENED + 1 :]):
        outs = (out_shape, env_shape, env_shape, trace_shape)
        if run[1] == width:
            outs += (((2, 2, 2), F32, pltpu.VMEM),)
        final, env, middle, traces, *totals = call(
            functools.partial(next_kernel, width, run),
            "run_%d" % run[0],
            (steps,),
            tuple((a, True) for a in (t0, t1, radius, traces, buffer, env, middle)) + ((final, False),),
            outs,
            stage,
            {6: 1, 7: 2, 8: 0},
        )
    return final, totals[0] + across(totals[0])


def solution(mesh):
    placed = (
        P(("grp", "site"), None, "sec", None, None),
        P("grp", None, None),
        P(),
        P(("grp", "site"), None),
        P("grp", "sec", None),
    )
    return jax.shard_map(
        shards,
        mesh=mesh,
        in_specs=placed,
        out_specs=(P(("grp", "site"), None, "sec", None, None), P(("grp", "site"), None, None)),
        check_vma=False,
    )
```

```python
import functools

import jax
import jax.numpy as jnp
from jax import lax
from jax.experimental import pallas as pl
from jax.experimental.pallas import tpu as pltpu
from jax.sharding import PartitionSpec as P

F32 = jnp.float32
BF16 = jnp.bfloat16
REACH = 4
HALO = 2
class Place:
    def __init__(self, width, steps):
        self.core = lax.axis_index("sec")
        self.pair = lax.axis_index("site")
        self.width = width
        self.steps = steps

    def local(self, b):
        return jnp.where(self.core == 0, self.width - 1 - b, b)


def dot(a, b):
    return jnp.dot(a, b, preferred_element_type=F32)


def dot_t(a, b):
    return lax.dot_general(a, b, (((0,), (0,)), ((), ())), preferred_element_type=F32)


def diagonal_row(block):
    half = block.shape[0] // 2
    row = lax.broadcasted_iota(jnp.int32, (half, half), 0)
    col = lax.broadcasted_iota(jnp.int32, (half, half), 1)
    parts = [
        jnp.sum(jnp.where(row == col, block[at : at + half, at : at + half], 0.0), axis=0, keepdims=True)
        for at in (0, half)
    ]
    return jnp.concatenate(parts, axis=1)


def pack(first, second):
    half = first.shape[0] // 2
    row = lax.broadcasted_iota(jnp.int32, (half, half), 0)
    col = lax.broadcasted_iota(jnp.int32, (half, half), 1)
    upper = row <= col

    def mixed(at):
        cut = slice(at, at + half)
        return jnp.where(upper, first[cut, cut], second[cut, cut])

    top = jnp.concatenate([mixed(0), first[:half, half:]], axis=1)
    bottom = jnp.concatenate([second[half:, :half], mixed(half)], axis=1)
    return jnp.concatenate([top, bottom], axis=0).astype(BF16)


def unpack(packed, diagonal, valid):
    half = packed.shape[0] // 2
    packed = jnp.where(valid, packed, jnp.zeros_like(packed))
    diagonal = jnp.where(valid, diagonal.astype(F32), 0.0)
    turned = packed.T
    row = lax.broadcasted_iota(jnp.int32, (half, half), 0)
    col = lax.broadcasted_iota(jnp.int32, (half, half), 1)

    def corners(at):
        cut = slice(at, at + half)
        straight, mirrored = packed[cut, cut].astype(F32), turned[cut, cut].astype(F32)
        low = jnp.where(row <= col, straight, mirrored)
        high = jnp.where(row == col, diagonal[:, cut], jnp.where(row < col, mirrored, straight))
        return low.astype(BF16), high.astype(BF16)

    def whole(north, ne, sw, south):
        top = jnp.concatenate([north, ne], axis=1)
        bottom = jnp.concatenate([sw, south], axis=1)
        return jnp.concatenate([top, bottom], axis=0)

    north, south = corners(0), corners(half)
    first = whole(north[0], packed[:half, half:], turned[half:, :half], south[0])
    second = whole(north[1], turned[:half, half:], packed[half:, :half], south[1])
    return first, second


def advance(env, slots, blocks, weight=None):
    size = blocks.shape[-1]
    middles = []
    for state in range(2):
        turned = blocks[state].T
        halves = []
        for insert in range(2):
            part = dot(turned, env[slots[state], insert * size : (insert + 1) * size])
            if weight is not None:
                part = part * weight[insert][state]
            halves.append(part.astype(BF16))
        middles.append(jnp.concatenate(halves, axis=0))
    both = dot(jnp.concatenate(middles, axis=1), blocks.reshape(2 * size, size))
    return both[:size], both[size:]


def squares(place, blocks, weight, b):
    terms = [dot(blocks[state].T, blocks[state]) for state in range(2)]
    out = []
    for insert in range(2):
        total = 0.0
        for state in range(2):
            inside = b + place.steps[state] < place.width
            total = total + jnp.where(inside, weight[insert][state], 0.0) * terms[state]
        out.append(total)
    return out


def fill_steps(place, sources, steps):
    middle = sources.shape[2] // 2
    for site in range(2):
        charge = sources[2 * place.pair + site, 0, middle] - middle + 1
        for state in range(2):
            steps[2 * site + state] = (2 * place.core - 1) * (charge + 2 * state - 1)


def fill_weights(operators, insert_at, weights):
    for which in range(2):
        for k in range(2):
            for s in range(2):
                weights[which, 2 * k + s] = jnp.where(insert_at[0, k] == which, operators[k, s], 1.0)


def weights_at(weights, which):
    return [[weights[which, 2 * k + s] for s in range(2)] for k in range(2)]


def add_traces(place, traces, at, site, b, parts, radius):
    row = radius[place.local(b), pl.ds(2 * place.pair + site, 1)]
    for k in range(2):
        traces[at + k : at + k + 1] += diagonal_row(parts[k].astype(BF16).astype(F32)) * (row * row)


def slots_of(place, site, b):
    return [REACH + b + place.steps[2 * site + state] for state in range(2)]


def store_env(env, slot, parts):
    size = parts[0].shape[0]
    for k in range(2):
        env[slot, k * size : (k + 1) * size] = parts[k].astype(BF16)


def send_one(place, env, t1, weight, traces, radius, sent, lo, b):
    parts = advance(env, slots_of(place, 1, b), t1[b], weight)
    size = parts[0].shape[0]
    sent[(b - lo) * size : (b - lo + 1) * size] = pack(*parts)
    add_traces(place, traces, 4, 1, b, parts, radius)
    return diagonal_row(parts[1])


def send_rows(sent, rows):
    count, size = len(rows), rows[0].shape[1]
    rows = rows + [jnp.zeros((16 - count, size), F32)]
    sent[count * size : count * size + 16] = jnp.concatenate(rows, axis=0).astype(BF16)


def send(place, env, t1, weight, traces, radius, sent, run):
    send_rows(sent, [send_one(place, env, t1, weight, traces, radius, sent, run[0], b) for b in range(*run)])


def take(place, buffer, i, count, env, slot):
    size = buffer.shape[1]
    diagonal = buffer[count * size : count * size + 16][i : i + 1]
    store_env(env, slot, unpack(buffer[i * size : (i + 1) * size], diagonal, place.pair > 0))


class Loads:
    def __init__(self):
        self.waiting = {}

    def start(self, key, source, target, sem):
        copy = pltpu.make_async_copy(source, target, sem)
        copy.start()
        self.waiting[key] = copy

    def wait(self, *keys):
        for key in keys:
            if key in self.waiting:
                self.waiting.pop(key).wait()


def first_kernel(width, run, sources, operators, insert_at, tensors, schmidt,
                 sent, edge, env, t0, t1, radius, traces, steps, weights, sources_here, operators_here, inserts_here, sems):
    place = Place(width, steps)
    lo, hi = run
    loads = Loads()
    loads.start("sources", sources, sources_here, sems.at[1, 0])
    loads.start("operators", operators, operators_here, sems.at[1, 1])
    loads.start("insert_at", insert_at, inserts_here, sems.at[1, width])
    near = list(range(hi + HALO))
    for b in near:
        loads.start(("t0", b), tensors.at[0, :, place.local(b)], t0.at[b], sems.at[0, b])
    for b in range(lo, hi):
        loads.start(("t1", b), tensors.at[1, :, place.local(b)], t1.at[b], sems.at[1, b])
    loads.start("radius", schmidt, radius, sems.at[0, width])
    traces[...] = jnp.zeros_like(traces)
    env[REACH + width :] = jnp.zeros_like(env[REACH + width :])
    loads.wait("sources", "operators", "insert_at")
    fill_steps(place, sources_here, steps)
    fill_weights(operators_here, inserts_here, weights)
    u, v = weights_at(weights, 0), weights_at(weights, 1)
    for group in [near]:
        for b in group:
            loads.wait(("t0", b))
        for b in group:
            parts = squares(place, t0[b], u, b)
            store_env(env, REACH + b, parts)
            if b < HALO:
                store_env(edge, HALO - 1 - b, parts)
                edge[2 * HALO - 1 - b] = t0[b].reshape(edge.shape[1:])
    for b in range(lo, hi):
        loads.wait(("t1", b))
    loads.wait("radius")
    send(place, env, t1, v, traces, radius, sent, run)


def second_kernel(width, first_run, runs, steps, weights, tensors, old_env, halo, old_t0, old_t1, radius,
                  old_traces, *rest):
    env, t0, t1, sents, (traces, sems) = *rest[:3], rest[3:-2], rest[-2:]
    place = Place(width, steps)
    size = t0.shape[-1]
    lo, hi = first_run
    late = [b for b in range(width) if not lo - HALO <= b < hi + HALO]
    order = [b for run in runs for b in range(*run)]
    loads = Loads()
    for b in late:
        loads.start(("t0", b), tensors.at[0, :, place.local(b)], t0.at[b], sems.at[0, b])
    for b in order:
        loads.start(("t1", b), tensors.at[1, :, place.local(b)], t1.at[b], sems.at[1, b])
    u, v = weights_at(weights, 0), weights_at(weights, 1)
    traces[...] = old_traces[...]
    for i in range(HALO):
        env[REACH - HALO + i] = halo[i]
    for b in range(width):
        if b in late:
            loads.wait(("t0", b))
            parts = squares(place, t0[b], u, b)
            store_env(env, REACH + b, parts)
        else:
            parts = [env[REACH + b, k * size : (k + 1) * size] for k in range(2)]
        add_traces(place, traces, 0, 0, b, parts, radius)
    for b in order:
        loads.wait(("t1", b))
    for run, sent in zip(runs, sents):
        send(place, env, t1, v, traces, radius, sent, run)


def open_kernel(width, runs, steps, *rest):
    buffers, (env, piece) = rest[: len(runs)], rest[len(runs) :]
    place = Place(width, steps)
    env[REACH + width :] = jnp.zeros_like(env[REACH + width :])
    for (lo, hi), buffer in zip(runs, buffers):
        for b in range(lo, hi):
            take(place, buffer, b - lo, hi - lo, env, REACH + b)
    size = buffers[0].shape[1]
    piece[: HALO * size] = buffers[0][: HALO * size]
    piece[HALO * size :] = buffers[0][(runs[0][1] - runs[0][0]) * size :]


def middle_blocks(place, todo, env, middle, t0, traces, radius):
    for b in range(*todo):
        parts = advance(env, slots_of(place, 0, b), t0[b])
        store_env(middle, REACH + b, parts)
        add_traces(place, traces, 2, 0, b, parts, radius)


def final_blocks(place, todo, middle, t1, traces, radius, stage, out, sems):
    stores = Loads()
    for b in range(*todo):
        parts = advance(middle, slots_of(place, 1, b), t1[b])
        for k in range(2):
            stage[b, k] = parts[k].astype(BF16)
        stores.start(b, stage.at[b], out.at[0, :, place.local(b)], sems.at[b])
        add_traces(place, traces, 6, 1, b, parts, radius)
    return stores


def edge_kernel(width, known, steps, t0, t1, halo, radius, old_traces, old_env, ours, *rest):
    beyond, (out, env, middle, traces, stage, sems) = rest[:2], rest[2:]
    place = Place(width, steps)
    traces[...] = old_traces[...]
    middle[REACH + width :] = jnp.zeros_like(middle[REACH + width :])
    for i in range(HALO):
        take(place, ours, i, HALO, env, REACH + i)
        for j in range(2):
            take(place, beyond[j], i, HALO, env, REACH - 1 - i - HALO * j)
    for i in range(HALO):
        blocks = halo[HALO + i].reshape(t0.shape[1:])
        store_env(middle, REACH - HALO + i, advance(env, slots_of(place, 0, i - HALO), blocks))
    middle_blocks(place, (0, known - HALO), env, middle, t0, traces, radius)
    last = (0, known - 2 * HALO)
    final_blocks(place, last, middle, t1, traces, radius, stage, out, sems).wait(*range(*last))


def next_kernel(width, run, steps, t0, t1, radius, old_traces, buffer, old_env, old_middle, old_out,
                out, env, middle, traces, *rest):
    totals, (stage, sems) = rest[:-2], rest[-2:]
    place = Place(width, steps)
    lo, hi = run
    upto = (width, width) if hi == width else (hi - HALO, hi - 2 * HALO)
    for b in range(lo, hi):
        take(place, buffer, b - lo, hi - lo, env, REACH + b)
    traces[...] = old_traces[...]
    middle_blocks(place, (lo - HALO, upto[0]), env, middle, t0, traces, radius)
    last = (lo - 2 * HALO, upto[1])
    stores = final_blocks(place, last, middle, t1, traces, radius, stage, out, sems)
    for total in totals:
        sums = jnp.sum(traces[...], axis=1, keepdims=True)
        for j in range(2):
            for t in range(2):
                at = 4 * j + 2 * t
                total[j, t : t + 1] = jnp.concatenate([sums[at : at + 1], sums[at + 1 : at + 2]], axis=1)
    stores.wait(*range(*last))


SMEM = pl.BlockSpec(memory_space=pltpu.SMEM)
VMEM = pl.BlockSpec(memory_space=pltpu.VMEM)
HBM = pl.BlockSpec(memory_space=pl.ANY)
PARAMS = pltpu.CompilerParams(vmem_limit_bytes=28 * 2**20)
RUNS = ((2, 5), (5, 7), (0, 2), (7, 10))
OPENED = 2


def call(kernel, name, scalars, arrays, outs, scratch=(), aliases=None):
    specs = {pltpu.VMEM: VMEM, pltpu.SMEM: SMEM, pltpu.HBM: HBM}
    where = [pltpu.SMEM] * len(scalars) + [pltpu.VMEM if near else pltpu.HBM for _, near in arrays]
    values = [*scalars, *[a for a, _ in arrays]]
    return pl.pallas_call(
        kernel,
        out_shape=tuple(memory(s, d) for s, d, memory in outs),
        in_specs=[specs[w] for w in where],
        out_specs=tuple(specs[memory] for _, _, memory in outs),
        scratch_shapes=list(scratch),
        compiler_params=PARAMS,
        input_output_aliases={} if aliases is None else aliases,
        name=name,
    )(*[pltpu.with_memory_space_constraint(a, w) for a, w in zip(values, where)])


def shards(tensors, sources, operators, insert_at, schmidt):
    width, size = tensors.shape[2], tensors.shape[-1]
    pairs = lax.axis_size("site")
    ring = [(i, (i + 1) % pairs) for i in range(pairs)]
    swap = [(0, 1), (1, 0)]
    schmidt = jnp.swapaxes(schmidt, 0, 1)

    def message(run):
        return ((run[1] - run[0]) * size + 16, size), BF16, pltpu.VMEM

    trace_shape = ((8, size), F32, pltpu.VMEM)
    env_shape = ((width + REACH + HALO, 2 * size, size), BF16, pltpu.VMEM)
    tensor_shape = ((width, 2, size, size), BF16, pltpu.VMEM)
    radius_shape = (schmidt.shape, F32, pltpu.VMEM)
    out_shape = ((1, 2, width, size, size), BF16, pltpu.HBM)
    stage = [pltpu.VMEM((width, 2, size, size), BF16), pltpu.SemaphoreType.DMA((width,))]

    def across(array):
        return lax.ppermute(array, "sec", swap)

    sent, edge, env, t0, t1, radius, traces, steps, weights = call(
        functools.partial(first_kernel, width, RUNS[0]),
        "anchor",
        (),
        tuple((a, False) for a in (sources, operators, insert_at, tensors, schmidt)),
        (
            message(RUNS[0]),
            ((2 * HALO, 2 * size, size), BF16, pltpu.VMEM),
            env_shape,
            tensor_shape,
            tensor_shape,
            radius_shape,
            trace_shape,
            ((4,), jnp.int32, pltpu.SMEM),
            ((2, 4), F32, pltpu.SMEM),
        ),
        [pltpu.SMEM(a.shape, a.dtype) for a in (sources, operators, insert_at)] + [pltpu.SemaphoreType.DMA((2, width + 1))],
    )
    halo = across(edge)
    got = [lax.ppermute(sent, "site", ring)]
    env, t0, t1, *sents, traces = call(
        functools.partial(second_kernel, width, RUNS[0], RUNS[1:]),
        "anchor_rest",
        (steps, weights),
        ((tensors, False),) + tuple((a, True) for a in (env, halo, t0, t1, radius, traces)),
        (env_shape, tensor_shape, tensor_shape) + tuple(message(r) for r in RUNS[1:]) + (trace_shape,),
        [pltpu.SemaphoreType.DMA((2, width))],
        {3: 0, 5: 1, 6: 2},
    )
    got += [lax.ppermute(s, "site", ring[:-1]) for s in sents]
    env, piece = call(
        functools.partial(open_kernel, width, RUNS[:OPENED]),
        "first_runs",
        (steps,),
        tuple((a, True) for a in got[:OPENED]),
        (env_shape, message(RUNS[OPENED])),
    )
    ours, env = lax.optimization_barrier((got[OPENED], env))
    final, env, middle, traces = call(
        functools.partial(edge_kernel, width, RUNS[OPENED - 1][1]),
        "edge",
        (steps,),
        tuple((a, True) for a in (t0, t1, halo, radius, traces, env, ours, across(ours), across(piece))),
        (out_shape, env_shape, env_shape, trace_shape),
        stage,
        {6: 1},
    )
    for run, buffer in zip(RUNS[OPENED + 1 :], got[OPENED + 1 :]):
        outs = (out_shape, env_shape, env_shape, trace_shape)
        if run[1] == width:
            outs += (((2, 2, 2), F32, pltpu.VMEM),)
        final, env, middle, traces, *totals = call(
            functools.partial(next_kernel, width, run),
            "run_%d" % run[0],
            (steps,),
            tuple((a, True) for a in (t0, t1, radius, traces, buffer, env, middle)) + ((final, False),),
            outs,
            stage,
            {6: 1, 7: 2, 8: 0},
        )
    return final, totals[0] + across(totals[0])


def solution(mesh):
    placed = (
        P(("grp", "site"), None, "sec", None, None),
        P("grp", None, None),
        P(),
        P(("grp", "site"), None),
        P("grp", "sec", None),
    )
    return jax.shard_map(
        shards,
        mesh=mesh,
        in_specs=placed,
        out_specs=(P(("grp", "site"), None, "sec", None, None), P(("grp", "site"), None, None)),
        check_vma=False,
    )
```

```python
import functools

import jax
import jax.numpy as jnp
from jax import lax
from jax.experimental import pallas as pl
from jax.experimental.pallas import tpu as pltpu
from jax.sharding import PartitionSpec as P

F32 = jnp.float32
BF16 = jnp.bfloat16
REACH = 4
HALO = 2
EXTRA = 16
class Place:
    def __init__(self, width, steps):
        self.core = lax.axis_index("sec")
        self.pair = lax.axis_index("site")
        self.width = width
        self.steps = steps

    def local(self, b):
        return jnp.where(self.core == 0, self.width - 1 - b, b)


def dot(a, b):
    return jnp.dot(a, b, preferred_element_type=F32)


def dot_t(a, b):
    return lax.dot_general(a, b, (((0,), (0,)), ((), ())), preferred_element_type=F32)


def diagonal_row(block):
    half = block.shape[0] // 2
    row = lax.broadcasted_iota(jnp.int32, (half, half), 0)
    col = lax.broadcasted_iota(jnp.int32, (half, half), 1)
    parts = [
        jnp.sum(jnp.where(row == col, block[at : at + half, at : at + half], 0.0), axis=0, keepdims=True)
        for at in (0, half)
    ]
    return jnp.concatenate(parts, axis=1)


def pack(first, second):
    half = first.shape[0] // 2
    row = lax.broadcasted_iota(jnp.int32, (half, half), 0)
    col = lax.broadcasted_iota(jnp.int32, (half, half), 1)
    upper = row <= col

    def mixed(at):
        cut = slice(at, at + half)
        return jnp.where(upper, first[cut, cut], second[cut, cut])

    top = jnp.concatenate([mixed(0), first[:half, half:]], axis=1)
    bottom = jnp.concatenate([second[half:, :half], mixed(half)], axis=1)
    return jnp.concatenate([top, bottom], axis=0).astype(BF16)


def unpack(packed, diagonal, valid):
    half = packed.shape[0] // 2
    packed = jnp.where(valid, packed, jnp.zeros_like(packed))
    diagonal = jnp.where(valid, diagonal.astype(F32), 0.0)
    turned = packed.T
    row = lax.broadcasted_iota(jnp.int32, (half, half), 0)
    col = lax.broadcasted_iota(jnp.int32, (half, half), 1)

    def corners(at):
        cut = slice(at, at + half)
        straight, mirrored = packed[cut, cut].astype(F32), turned[cut, cut].astype(F32)
        low = jnp.where(row <= col, straight, mirrored)
        high = jnp.where(row == col, diagonal[:, cut], jnp.where(row < col, mirrored, straight))
        return low.astype(BF16), high.astype(BF16)

    def whole(north, ne, sw, south):
        top = jnp.concatenate([north, ne], axis=1)
        bottom = jnp.concatenate([sw, south], axis=1)
        return jnp.concatenate([top, bottom], axis=0)

    north, south = corners(0), corners(half)
    first = whole(north[0], packed[:half, half:], turned[half:, :half], south[0])
    second = whole(north[1], turned[:half, half:], packed[half:, :half], south[1])
    return first, second


def advance(env, slots, blocks, weight=None):
    size = blocks[0].shape[-1]
    middles = []
    for state in range(2):
        turned = blocks[state].T
        halves = []
        for insert in range(2):
            part = dot(turned, env[slots[state], insert * size : (insert + 1) * size])
            if weight is not None:
                part = part * weight[insert][state]
            halves.append(part.astype(BF16))
        middles.append(jnp.concatenate(halves, axis=0))
    both = dot(jnp.concatenate(middles, axis=1), jnp.concatenate(blocks, axis=0))
    return both[:size], both[size:]


def one_state(place, env, site, state, tensors, b):
    size = env.shape[-1]
    block = tensors[state, place.local(b)]
    slot = REACH + b + place.steps[2 * site + state]
    turned = block.T
    halves = [dot(turned, env[slot, k * size : (k + 1) * size]).astype(BF16) for k in range(2)]
    return dot(jnp.concatenate(halves, axis=0), block)


def begin(place, todo, env, site, tensors, partial):
    for i, b in enumerate(range(*todo)):
        partial[i] = one_state(place, env, site, 1 - place.core, tensors, b)


def complete(place, i, b, env, site, tensors, partial):
    both = partial[i] + one_state(place, env, site, place.core, tensors, b)
    size = env.shape[-1]
    return both[:size], both[size:]


def squares(place, blocks, weight, b):
    terms = [dot(blocks[state].T, blocks[state]) for state in range(2)]
    out = []
    for insert in range(2):
        total = 0.0
        for state in range(2):
            inside = b + place.steps[state] < place.width
            total = total + jnp.where(inside, weight[insert][state], 0.0) * terms[state]
        out.append(total)
    return out


def fill_steps(place, sources, steps):
    middle = sources.shape[2] // 2
    for site in range(2):
        charge = sources[2 * place.pair + site, 0, middle] - middle + 1
        for state in range(2):
            steps[2 * site + state] = (2 * place.core - 1) * (charge + 2 * state - 1)


def fill_weights(operators, insert_at, weights):
    for which in range(2):
        for k in range(2):
            for s in range(2):
                weights[which, 2 * k + s] = jnp.where(insert_at[0, k] == which, operators[k, s], 1.0)


def weights_at(weights, which):
    return [[weights[which, 2 * k + s] for s in range(2)] for k in range(2)]


def add_traces(place, traces, at, site, b, parts, radius):
    row = radius[place.local(b), pl.ds(2 * place.pair + site, 1)]
    for k in range(2):
        traces[at + k : at + k + 1] += diagonal_row(parts[k].astype(BF16).astype(F32)) * (row * row)


def slots_of(place, site, b):
    return [REACH + b + place.steps[2 * site + state] for state in range(2)]


def store_env(env, slot, parts):
    size = parts[0].shape[0]
    for k in range(2):
        env[slot, k * size : (k + 1) * size] = parts[k].astype(BF16)


def blocks_of(place, tensors, b):
    return [tensors[state, place.local(b)] for state in range(2)]


def send(place, env, t1, weight, traces, radius, sent, run):
    rows = []
    for b in range(*run):
        parts = advance(env, slots_of(place, 1, b), blocks_of(place, t1, b), weight)
        size = parts[0].shape[0]
        sent[(b - run[0]) * size : (b - run[0] + 1) * size] = pack(*parts)
        add_traces(place, traces, 4, 1, b, parts, radius)
        rows.append(diagonal_row(parts[1]))
    return rows


def send_rows(sent, rows):
    rows = jnp.concatenate(rows, axis=0)
    rows = jnp.concatenate([rows, jnp.zeros((EXTRA - rows.shape[0], rows.shape[1]), F32)], axis=0)
    sent[sent.shape[0] - EXTRA :] = rows.astype(BF16)


def below(buffer):
    return buffer[buffer.shape[0] - EXTRA :]


def take(place, buffer, i, diagonals, row, env, slot):
    size = buffer.shape[1]
    store_env(env, slot, unpack(buffer[i * size : (i + 1) * size], diagonals[row : row + 1], place.pair > 0))


class Loads:
    def __init__(self):
        self.waiting = {}

    def start(self, key, source, target, sem):
        copy = pltpu.make_async_copy(source, target, sem)
        copy.start()
        self.waiting[key] = copy

    def tensors(self, place, source, target, site, lo, hi, sem):
        at = pl.ds(jnp.where(place.core == 0, place.width - hi, lo), hi - lo)
        self.start((site, lo), source.at[site, :, at], target.at[:, at], sem)

    def wait(self, *keys):
        for key in keys:
            if key in self.waiting:
                self.waiting.pop(key).wait()


def first_kernel(width, run, sources, operators, insert_at, tensors, schmidt,
                 sent, edge, env, t0, t1, radius, traces, steps, weights, sources_here, operators_here, inserts_here, sems):
    place = Place(width, steps)
    lo, hi = run
    loads = Loads()
    loads.start("sources", sources, sources_here, sems.at[0])
    loads.start("operators", operators, operators_here, sems.at[1])
    loads.start("insert_at", insert_at, inserts_here, sems.at[2])
    near = hi + HALO
    loads.tensors(place, tensors, t0, 0, 0, near, sems.at[3])
    loads.tensors(place, tensors, t1, 1, lo, hi, sems.at[4])
    loads.start("radius", schmidt, radius, sems.at[5])
    traces[...] = jnp.zeros_like(traces)
    env[REACH + width :] = jnp.zeros_like(env[REACH + width :])
    loads.wait("sources", "operators", "insert_at")
    fill_steps(place, sources_here, steps)
    fill_weights(operators_here, inserts_here, weights)
    u, v = weights_at(weights, 0), weights_at(weights, 1)
    loads.wait((0, 0))
    for b in range(near):
        blocks = blocks_of(place, t0, b)
        parts = squares(place, blocks, u, b)
        store_env(env, REACH + b, parts)
        if b < HALO:
            store_env(edge, HALO - 1 - b, parts)
            edge[2 * HALO - 1 - b] = jnp.concatenate(blocks, axis=0)
    loads.wait((1, lo), "radius")
    send_rows(sent, send(place, env, t1, v, traces, radius, sent, run))


def second_kernel(width, first_run, runs, steps, weights, tensors, old_env, halo, old_t0, old_t1, radius,
                  old_traces, *rest):
    env, t0, t1, sents, (traces, sems) = *rest[:3], rest[3:-2], rest[-2:]
    place = Place(width, steps)
    size = t0.shape[-1]
    lo, hi = first_run
    known = hi + HALO
    loads = Loads()
    loads.tensors(place, tensors, t0, 0, known, width, sems.at[0])
    loads.tensors(place, tensors, t1, 1, hi, width, sems.at[1])
    loads.tensors(place, tensors, t1, 1, 0, lo, sems.at[2])
    u, v = weights_at(weights, 0), weights_at(weights, 1)
    traces[...] = old_traces[...]
    for i in range(HALO):
        env[REACH - HALO + i] = halo[i]
    for b in range(known):
        parts = [env[REACH + b, k * size : (k + 1) * size] for k in range(2)]
        add_traces(place, traces, 0, 0, b, parts, radius)
    loads.wait((0, known))
    for b in range(known, width):
        parts = squares(place, blocks_of(place, t0, b), u, b)
        store_env(env, REACH + b, parts)
        add_traces(place, traces, 0, 0, b, parts, radius)
    loads.wait((1, hi), (1, 0))
    rows = []
    for run, sent in zip(runs, sents):
        rows += send(place, env, t1, v, traces, radius, sent, run)
    send_rows(sents[0], rows)


def middle_blocks(place, todo, env, middle, t0, traces, radius, partial=None):
    for i, b in enumerate(range(*todo)):
        if partial is not None and i < HALO:
            parts = complete(place, i, b, env, 0, t0, partial)
        else:
            parts = advance(env, slots_of(place, 0, b), blocks_of(place, t0, b))
        store_env(middle, REACH + b, parts)
        add_traces(place, traces, 2, 0, b, parts, radius)


def open_kernel(width, run, steps, first, env, middle, piece):
    place = Place(width, steps)
    size = first.shape[1]
    for array in (env, middle):
        array[REACH + width :] = jnp.zeros_like(array[REACH + width :])
    lo, hi = run
    for b in range(lo, hi):
        take(place, first, b - lo, below(first), b - lo, env, REACH + b)
    piece[: HALO * size] = first[: HALO * size]
    piece[HALO * size :] = below(first)


def final_blocks(place, todo, middle, t1, traces, radius, stage, out, sems, partial=None):
    stores = Loads()
    for i, b in enumerate(range(*todo)):
        if partial is not None and i < HALO:
            parts = complete(place, i, b, middle, 1, t1, partial)
        else:
            parts = advance(middle, slots_of(place, 1, b), blocks_of(place, t1, b))
        for k in range(2):
            stage[b, k] = parts[k].astype(BF16)
        stores.start(b, stage.at[b], out.at[0, :, place.local(b)], sems.at[b])
        add_traces(place, traces, 6, 1, b, parts, radius)
    return stores


def edge_kernel(width, known, steps, t0, t1, halo, radius, old_traces, old_env, old_middle, ours, near, far,
                out, env, middle, traces, partial0, partial1, stage, sems):
    place = Place(width, steps)
    size = t0.shape[-1]
    traces[...] = old_traces[...]
    for i in range(HALO):
        take(place, ours, i, below(ours), i, env, REACH + i)
        take(place, near, i, below(near), i, env, REACH - 1 - i)
        take(place, far, i, below(far), i, env, REACH - 1 - HALO - i)
    for i in range(HALO):
        blocks = [halo[HALO + i, state * size : (state + 1) * size] for state in range(2)]
        store_env(middle, REACH - HALO + i, advance(env, slots_of(place, 0, i - HALO), blocks))
    middle_blocks(place, (0, known - HALO), env, middle, t0, traces, radius)
    last = (0, known - 2 * HALO)
    stores = final_blocks(place, last, middle, t1, traces, radius, stage, out, sems)
    begin(place, (known - HALO, known), env, 0, t0, partial0)
    begin(place, (last[1], last[1] + HALO), middle, 1, t1, partial1)
    stores.wait(*range(*last))


def next_kernel(width, run, row, steps, t0, t1, radius, old_traces, ours, buffer, old_partial0, old_partial1, old_env, old_middle,
                old_out, out, env, middle, traces, *rest):
    results, (stage, sems) = rest[:-2], rest[-2:]
    place = Place(width, steps)
    lo, hi = run
    for b in range(lo, hi):
        take(place, buffer, b - lo, below(ours), row + b - lo, env, REACH + b)
    traces[...] = old_traces[...]
    ends = hi == width
    upto = width if ends else hi - HALO
    middle_blocks(place, (lo - HALO, upto), env, middle, t0, traces, radius, old_partial0)
    last = (lo - 2 * HALO, width if ends else upto - HALO)
    stores = final_blocks(place, last, middle, t1, traces, radius, stage, out, sems, old_partial1)
    if ends:
        (totals,) = results
        sums = jnp.sum(traces[...], axis=1, keepdims=True)
        for j in range(2):
            for t in range(2):
                at = 4 * j + 2 * t
                totals[j, t : t + 1] = jnp.concatenate([sums[at : at + 1], sums[at + 1 : at + 2]], axis=1)
    else:
        begin(place, (upto, hi), env, 0, t0, results[0])
        begin(place, (last[1], upto), middle, 1, t1, results[1])
    stores.wait(*range(*last))


SMEM = pl.BlockSpec(memory_space=pltpu.SMEM)
VMEM = pl.BlockSpec(memory_space=pltpu.VMEM)
HBM = pl.BlockSpec(memory_space=pl.ANY)
PARAMS = pltpu.CompilerParams(vmem_limit_bytes=28 * 2**20)
RUNS = ((2, 5), (0, 2), (5, 8), (8, 10))


def call(kernel, name, scalars, arrays, outs, scratch=(), aliases=None):
    specs = {pltpu.VMEM: VMEM, pltpu.SMEM: SMEM, pltpu.HBM: HBM}
    where = [pltpu.SMEM] * len(scalars) + [pltpu.VMEM if near else pltpu.HBM for _, near in arrays]
    values = [*scalars, *[a for a, _ in arrays]]
    return pl.pallas_call(
        kernel,
        out_shape=tuple(memory(s, d) for s, d, memory in outs),
        in_specs=[specs[w] for w in where],
        out_specs=tuple(specs[memory] for _, _, memory in outs),
        scratch_shapes=list(scratch),
        compiler_params=PARAMS,
        input_output_aliases={} if aliases is None else aliases,
        name=name,
    )(*[pltpu.with_memory_space_constraint(a, w) for a, w in zip(values, where)])


def shards(tensors, sources, operators, insert_at, schmidt):
    width, size = tensors.shape[2], tensors.shape[-1]
    pairs = lax.axis_size("site")
    ring = [(i, (i + 1) % pairs) for i in range(pairs)]
    swap = [(0, 1), (1, 0)]
    schmidt = jnp.swapaxes(schmidt, 0, 1)

    def message(run, extra=EXTRA):
        return ((run[1] - run[0]) * size + extra, size), BF16, pltpu.VMEM

    trace_shape = ((8, size), F32, pltpu.VMEM)
    env_shape = ((width + REACH + HALO, 2 * size, size), BF16, pltpu.VMEM)
    tensor_shape = ((2, width, size, size), BF16, pltpu.VMEM)
    partial_shape = ((HALO, 2 * size, size), F32, pltpu.VMEM)
    radius_shape = (schmidt.shape, F32, pltpu.VMEM)
    out_shape = ((1, 2, width, size, size), BF16, pltpu.HBM)
    stage = [pltpu.VMEM((width, 2, size, size), BF16), pltpu.SemaphoreType.DMA((width,))]

    def across(array):
        return lax.ppermute(array, "sec", swap)

    sent, edge, env, t0, t1, radius, traces, steps, weights = call(
        functools.partial(first_kernel, width, RUNS[0]),
        "anchor",
        (),
        tuple((a, False) for a in (sources, operators, insert_at, tensors, schmidt)),
        (
            message(RUNS[0]),
            ((2 * HALO, 2 * size, size), BF16, pltpu.VMEM),
            env_shape,
            tensor_shape,
            tensor_shape,
            radius_shape,
            trace_shape,
            ((4,), jnp.int32, pltpu.SMEM),
            ((2, 4), F32, pltpu.SMEM),
        ),
        [pltpu.SMEM(a.shape, a.dtype) for a in (sources, operators, insert_at)] + [pltpu.SemaphoreType.DMA((6,))],
    )
    halo = across(edge)
    got = [lax.ppermute(sent, "site", ring)]
    env, t0, t1, *sents, traces = call(
        functools.partial(second_kernel, width, RUNS[0], RUNS[1:]),
        "anchor_rest",
        (steps, weights),
        ((tensors, False),) + tuple((a, True) for a in (env, halo, t0, t1, radius, traces)),
        (env_shape, tensor_shape, tensor_shape) + (message(RUNS[1]), message(RUNS[2], 0), message(RUNS[3], 0)) + (trace_shape,),
        [pltpu.SemaphoreType.DMA((3,))],
        {3: 0, 5: 1, 6: 2},
    )
    got += [lax.ppermute(s, "site", ring[:-1]) for s in sents]
    env, middle, piece = call(
        functools.partial(open_kernel, width, RUNS[0]),
        "first_run",
        (steps,),
        ((got[0], True),),
        (env_shape, env_shape, message(RUNS[1])),
    )
    ours, env = lax.optimization_barrier((got[1], env))
    final, env, middle, traces, *partials = call(
        functools.partial(edge_kernel, width, RUNS[0][1]),
        "edge",
        (steps,),
        tuple((a, True) for a in (t0, t1, halo, radius, traces, env, middle, ours, across(ours), across(piece))),
        (out_shape, env_shape, env_shape, trace_shape, partial_shape, partial_shape),
        stage,
        {6: 1, 7: 2},
    )
    row = RUNS[1][1] - RUNS[1][0]
    for run, buffer in zip(RUNS[2:], got[2:]):
        results = (partial_shape, partial_shape) if run[1] < width else (((2, 2, 2), F32, pltpu.VMEM),)
        final, env, middle, traces, *partials = call(
            functools.partial(next_kernel, width, run, row),
            "run_%d" % run[0],
            (steps,),
            tuple((a, True) for a in (t0, t1, radius, traces, ours, buffer, *partials, env, middle)) + ((final, False),),
            (out_shape, env_shape, env_shape, trace_shape) + results,
            stage,
            {9: 1, 10: 2, 11: 0},
        )
        row += run[1] - run[0]
    (totals,) = partials
    return final, totals + across(totals)


def solution(mesh):
    placed = (
        P(("grp", "site"), None, "sec", None, None),
        P("grp", None, None),
        P(),
        P(("grp", "site"), None),
        P("grp", "sec", None),
    )
    return jax.shard_map(
        shards,
        mesh=mesh,
        in_specs=placed,
        out_specs=(P(("grp", "site"), None, "sec", None, None), P(("grp", "site"), None, None)),
        check_vma=False,
    )
```

```python
import functools

import jax
import jax.numpy as jnp
from jax import lax
from jax.experimental import pallas as pl
from jax.experimental.pallas import tpu as pltpu
from jax.sharding import PartitionSpec as P

F32 = jnp.float32
BF16 = jnp.bfloat16
REACH = 4
HALO = 2
EXTRA = 16
class Place:
    def __init__(self, width, steps):
        self.core = lax.axis_index("sec")
        self.pair = lax.axis_index("site")
        self.width = width
        self.steps = steps

    def local(self, b):
        return jnp.where(self.core == 0, self.width - 1 - b, b)


def dot(a, b):
    return jnp.dot(a, b, preferred_element_type=F32)


def dot_t(a, b):
    return lax.dot_general(a, b, (((0,), (0,)), ((), ())), preferred_element_type=F32)


def diagonal_row(block):
    half = block.shape[0] // 2
    row = lax.broadcasted_iota(jnp.int32, (half, half), 0)
    col = lax.broadcasted_iota(jnp.int32, (half, half), 1)
    parts = [
        jnp.sum(jnp.where(row == col, block[at : at + half, at : at + half], 0.0), axis=0, keepdims=True)
        for at in (0, half)
    ]
    return jnp.concatenate(parts, axis=1)


def pack(first, second):
    half = first.shape[0] // 2
    row = lax.broadcasted_iota(jnp.int32, (half, half), 0)
    col = lax.broadcasted_iota(jnp.int32, (half, half), 1)
    upper = row <= col

    def mixed(at):
        cut = slice(at, at + half)
        return jnp.where(upper, first[cut, cut], second[cut, cut])

    top = jnp.concatenate([mixed(0), first[:half, half:]], axis=1)
    bottom = jnp.concatenate([second[half:, :half], mixed(half)], axis=1)
    return jnp.concatenate([top, bottom], axis=0).astype(BF16)


def unpack(packed, diagonal, valid):
    half = packed.shape[0] // 2
    packed = jnp.where(valid, packed, jnp.zeros_like(packed))
    diagonal = jnp.where(valid, diagonal.astype(F32), 0.0)
    turned = packed.T
    row = lax.broadcasted_iota(jnp.int32, (half, half), 0)
    col = lax.broadcasted_iota(jnp.int32, (half, half), 1)

    def corners(at):
        cut = slice(at, at + half)
        straight, mirrored = packed[cut, cut].astype(F32), turned[cut, cut].astype(F32)
        low = jnp.where(row <= col, straight, mirrored)
        high = jnp.where(row == col, diagonal[:, cut], jnp.where(row < col, mirrored, straight))
        return low.astype(BF16), high.astype(BF16)

    def whole(north, ne, sw, south):
        top = jnp.concatenate([north, ne], axis=1)
        bottom = jnp.concatenate([sw, south], axis=1)
        return jnp.concatenate([top, bottom], axis=0)

    north, south = corners(0), corners(half)
    first = whole(north[0], packed[:half, half:], turned[half:, :half], south[0])
    second = whole(north[1], turned[:half, half:], packed[half:, :half], south[1])
    return first, second


def advance(env, slots, blocks, weight=None):
    size = blocks[0].shape[-1]
    middles = []
    for state in range(2):
        turned = blocks[state].T
        halves = []
        for insert in range(2):
            part = dot(turned, env[slots[state], insert * size : (insert + 1) * size])
            if weight is not None:
                part = part * weight[insert][state]
            halves.append(part.astype(BF16))
        middles.append(jnp.concatenate(halves, axis=0))
    both = dot(jnp.concatenate(middles, axis=1), jnp.concatenate(blocks, axis=0))
    return both[:size], both[size:]


def one_state(place, env, site, state, tensors, b):
    size = env.shape[-1]
    block = tensors[state, place.local(b)]
    slot = REACH + b + place.steps[2 * site + state]
    turned = block.T
    halves = [dot(turned, env[slot, k * size : (k + 1) * size]).astype(BF16) for k in range(2)]
    return dot(jnp.concatenate(halves, axis=0), block)


def early_state(place, site, b, known):
    nearer = 1 - place.core
    return jnp.where(b + place.steps[2 * site + nearer] < known, nearer, 1 - nearer)


def begin(place, todo, known, env, site, tensors, partial):
    for i, b in enumerate(range(*todo)):
        partial[i] = one_state(place, env, site, early_state(place, site, b, known), tensors, b)


def complete(place, i, b, known, env, site, tensors, partial):
    both = partial[i] + one_state(place, env, site, 1 - early_state(place, site, b, known), tensors, b)
    size = env.shape[-1]
    return both[:size], both[size:]


def squares(place, blocks, weight, b):
    terms = [dot(blocks[state].T, blocks[state]) for state in range(2)]
    out = []
    for insert in range(2):
        total = 0.0
        for state in range(2):
            inside = b + place.steps[state] < place.width
            total = total + jnp.where(inside, weight[insert][state], 0.0) * terms[state]
        out.append(total)
    return out


def fill_steps(place, sources, steps):
    middle = sources.shape[2] // 2
    for site in range(2):
        charge = sources[2 * place.pair + site, 0, middle] - middle + 1
        for state in range(2):
            steps[2 * site + state] = (2 * place.core - 1) * (charge + 2 * state - 1)


def fill_weights(operators, insert_at, weights):
    for which in range(2):
        for k in range(2):
            for s in range(2):
                weights[which, 2 * k + s] = jnp.where(insert_at[0, k] == which, operators[k, s], 1.0)


def weights_at(weights, which):
    return [[weights[which, 2 * k + s] for s in range(2)] for k in range(2)]


def add_traces(place, traces, at, site, b, parts, radius):
    row = radius[place.local(b), pl.ds(2 * place.pair + site, 1)]
    for k in range(2):
        traces[at + k : at + k + 1] += diagonal_row(parts[k].astype(BF16).astype(F32)) * (row * row)


def slots_of(place, site, b):
    return [REACH + b + place.steps[2 * site + state] for state in range(2)]


def store_env(env, slot, parts):
    size = parts[0].shape[0]
    for k in range(2):
        env[slot, k * size : (k + 1) * size] = parts[k].astype(BF16)


def blocks_of(place, tensors, b):
    return [tensors[state, place.local(b)] for state in range(2)]


def send(place, env, t1, weight, traces, radius, sent, run):
    rows = []
    for b in range(*run):
        parts = advance(env, slots_of(place, 1, b), blocks_of(place, t1, b), weight)
        size = parts[0].shape[0]
        sent[(b - run[0]) * size : (b - run[0] + 1) * size] = pack(*parts)
        add_traces(place, traces, 4, 1, b, parts, radius)
        rows.append(diagonal_row(parts[1]))
    return rows


def send_rows(sent, rows):
    rows = jnp.concatenate(rows, axis=0)
    rows = jnp.concatenate([rows, jnp.zeros((EXTRA - rows.shape[0], rows.shape[1]), F32)], axis=0)
    sent[sent.shape[0] - EXTRA :] = rows.astype(BF16)


def below(buffer):
    return buffer[buffer.shape[0] - EXTRA :]


def take(place, buffer, i, diagonals, row, env, slot):
    size = buffer.shape[1]
    store_env(env, slot, unpack(buffer[i * size : (i + 1) * size], diagonals[row : row + 1], place.pair > 0))


class Loads:
    def __init__(self):
        self.waiting = {}

    def start(self, key, source, target, sem):
        copy = pltpu.make_async_copy(source, target, sem)
        copy.start()
        self.waiting[key] = copy

    def tensors(self, place, source, target, site, lo, hi, sem):
        at = pl.ds(jnp.where(place.core == 0, place.width - hi, lo), hi - lo)
        self.start((site, lo), source.at[site, :, at], target.at[:, at], sem)

    def wait(self, *keys):
        for key in keys:
            if key in self.waiting:
                self.waiting.pop(key).wait()


def first_kernel(width, run, sources, operators, insert_at, tensors, schmidt,
                 sent, edge, env, t0, t1, radius, traces, steps, weights, sources_here, operators_here, inserts_here, sems):
    place = Place(width, steps)
    lo, hi = run
    loads = Loads()
    loads.start("sources", sources, sources_here, sems.at[0])
    loads.start("operators", operators, operators_here, sems.at[1])
    loads.start("insert_at", insert_at, inserts_here, sems.at[2])
    near = hi + HALO
    loads.tensors(place, tensors, t0, 0, 0, near, sems.at[3])
    loads.tensors(place, tensors, t1, 1, lo, hi, sems.at[4])
    loads.start("radius", schmidt, radius, sems.at[5])
    traces[...] = jnp.zeros_like(traces)
    env[REACH + width :] = jnp.zeros_like(env[REACH + width :])
    loads.wait("sources", "operators", "insert_at")
    fill_steps(place, sources_here, steps)
    fill_weights(operators_here, inserts_here, weights)
    u, v = weights_at(weights, 0), weights_at(weights, 1)
    loads.wait((0, 0))
    for b in range(near):
        blocks = blocks_of(place, t0, b)
        parts = squares(place, blocks, u, b)
        store_env(env, REACH + b, parts)
        if b < HALO:
            store_env(edge, HALO - 1 - b, parts)
            edge[2 * HALO - 1 - b] = jnp.concatenate(blocks, axis=0)
    loads.wait((1, lo), "radius")
    send_rows(sent, send(place, env, t1, v, traces, radius, sent, run))


def second_kernel(width, first_run, runs, steps, weights, tensors, old_env, halo, old_t0, old_t1, radius,
                  old_traces, *rest):
    env, t0, t1, sents, (traces, sems) = *rest[:3], rest[3:-2], rest[-2:]
    place = Place(width, steps)
    size = t0.shape[-1]
    lo, hi = first_run
    known = hi + HALO
    loads = Loads()
    loads.tensors(place, tensors, t0, 0, known, width, sems.at[0])
    loads.tensors(place, tensors, t1, 1, hi, width, sems.at[1])
    loads.tensors(place, tensors, t1, 1, 0, lo, sems.at[2])
    u, v = weights_at(weights, 0), weights_at(weights, 1)
    traces[...] = old_traces[...]
    for i in range(HALO):
        env[REACH - HALO + i] = halo[i]
    for b in range(known):
        parts = [env[REACH + b, k * size : (k + 1) * size] for k in range(2)]
        add_traces(place, traces, 0, 0, b, parts, radius)
    loads.wait((0, known))
    for b in range(known, width):
        parts = squares(place, blocks_of(place, t0, b), u, b)
        store_env(env, REACH + b, parts)
        add_traces(place, traces, 0, 0, b, parts, radius)
    loads.wait((1, hi), (1, 0))
    rows = []
    for run, sent in zip(runs, sents):
        rows += send(place, env, t1, v, traces, radius, sent, run)
    send_rows(sents[0], rows)


def middle_blocks(place, todo, env, middle, t0, traces, radius, partial=None, known=0):
    for i, b in enumerate(range(*todo)):
        if partial is not None and i < partial.shape[0]:
            parts = complete(place, i, b, known, env, 0, t0, partial)
        else:
            parts = advance(env, slots_of(place, 0, b), blocks_of(place, t0, b))
        store_env(middle, REACH + b, parts)
        add_traces(place, traces, 2, 0, b, parts, radius)


def open_kernel(width, run, steps, first, env, middle, piece):
    place = Place(width, steps)
    size = first.shape[1]
    for array in (env, middle):
        array[REACH + width :] = jnp.zeros_like(array[REACH + width :])
    lo, hi = run
    for b in range(lo, hi):
        take(place, first, b - lo, below(first), b - lo, env, REACH + b)
    piece[: HALO * size] = first[: HALO * size]
    piece[HALO * size :] = below(first)


def final_blocks(place, todo, middle, t1, traces, radius, stage, out, sems, partial=None, known=0):
    stores = Loads()
    for i, b in enumerate(range(*todo)):
        if partial is not None and i < partial.shape[0]:
            parts = complete(place, i, b, known, middle, 1, t1, partial)
        else:
            parts = advance(middle, slots_of(place, 1, b), blocks_of(place, t1, b))
        for k in range(2):
            stage[b, k] = parts[k].astype(BF16)
        stores.start(b, stage.at[b], out.at[0, :, place.local(b)], sems.at[b])
        add_traces(place, traces, 6, 1, b, parts, radius)
    return stores


def edge_kernel(width, known, steps, t0, t1, halo, radius, old_traces, old_env, old_middle, ours, near, far,
                out, env, middle, traces, partial0, partial1, stage, sems):
    place = Place(width, steps)
    size = t0.shape[-1]
    traces[...] = old_traces[...]
    for i in range(HALO):
        take(place, ours, i, below(ours), i, env, REACH + i)
        take(place, near, i, below(near), i, env, REACH - 1 - i)
        take(place, far, i, below(far), i, env, REACH - 1 - HALO - i)
    for i in range(HALO):
        blocks = [halo[HALO + i, state * size : (state + 1) * size] for state in range(2)]
        store_env(middle, REACH - HALO + i, advance(env, slots_of(place, 0, i - HALO), blocks))
    middle_blocks(place, (0, known - HALO), env, middle, t0, traces, radius)
    last = (0, known - 2 * HALO)
    stores = final_blocks(place, last, middle, t1, traces, radius, stage, out, sems)
    begin(place, (known - HALO, known), known, env, 0, t0, partial0)
    begin(place, (last[1], last[1] + HALO), known - HALO, middle, 1, t1, partial1)
    stores.wait(*range(*last))


def next_kernel(width, run, row, steps, t0, t1, radius, old_traces, ours, buffer, old_partial0, old_partial1, old_env, old_middle,
                old_out, out, env, middle, traces, *rest):
    results, (stage, sems) = rest[:-2], rest[-2:]
    place = Place(width, steps)
    lo, hi = run
    for b in range(lo, hi):
        take(place, buffer, b - lo, below(ours), row + b - lo, env, REACH + b)
    traces[...] = old_traces[...]
    ends = hi == width
    upto = width if ends else hi - HALO
    middle_blocks(place, (lo - HALO, upto), env, middle, t0, traces, radius, old_partial0, lo)
    last = (lo - 2 * HALO, width if ends else upto - HALO)
    stores = final_blocks(place, last, middle, t1, traces, radius, stage, out, sems, old_partial1, lo - HALO)
    if ends:
        (totals,) = results
        sums = jnp.sum(traces[...], axis=1, keepdims=True)
        for j in range(2):
            for t in range(2):
                at = 4 * j + 2 * t
                totals[j, t : t + 1] = jnp.concatenate([sums[at : at + 1], sums[at + 1 : at + 2]], axis=1)
    else:
        begin(place, (upto, upto + results[0].shape[0]), hi, env, 0, t0, results[0])
        begin(place, (last[1], upto), upto, middle, 1, t1, results[1])
    stores.wait(*range(*last))


SMEM = pl.BlockSpec(memory_space=pltpu.SMEM)
VMEM = pl.BlockSpec(memory_space=pltpu.VMEM)
HBM = pl.BlockSpec(memory_space=pl.ANY)
PARAMS = pltpu.CompilerParams(vmem_limit_bytes=28 * 2**20)
RUNS = ((2, 5), (0, 2), (5, 8), (8, 10))


def call(kernel, name, scalars, arrays, outs, scratch=(), aliases=None):
    specs = {pltpu.VMEM: VMEM, pltpu.SMEM: SMEM, pltpu.HBM: HBM}
    where = [pltpu.SMEM] * len(scalars) + [pltpu.VMEM if near else pltpu.HBM for _, near in arrays]
    values = [*scalars, *[a for a, _ in arrays]]
    return pl.pallas_call(
        kernel,
        out_shape=tuple(memory(s, d) for s, d, memory in outs),
        in_specs=[specs[w] for w in where],
        out_specs=tuple(specs[memory] for _, _, memory in outs),
        scratch_shapes=list(scratch),
        compiler_params=PARAMS,
        input_output_aliases={} if aliases is None else aliases,
        name=name,
    )(*[pltpu.with_memory_space_constraint(a, w) for a, w in zip(values, where)])


def shards(tensors, sources, operators, insert_at, schmidt):
    width, size = tensors.shape[2], tensors.shape[-1]
    pairs = lax.axis_size("site")
    ring = [(i, (i + 1) % pairs) for i in range(pairs)]
    swap = [(0, 1), (1, 0)]
    schmidt = jnp.swapaxes(schmidt, 0, 1)

    def message(run, extra=EXTRA):
        return ((run[1] - run[0]) * size + extra, size), BF16, pltpu.VMEM

    trace_shape = ((8, size), F32, pltpu.VMEM)
    env_shape = ((width + REACH + HALO, 2 * size, size), BF16, pltpu.VMEM)
    tensor_shape = ((2, width, size, size), BF16, pltpu.VMEM)
    partial_shape = ((HALO, 2 * size, size), F32, pltpu.VMEM)
    radius_shape = (schmidt.shape, F32, pltpu.VMEM)
    out_shape = ((1, 2, width, size, size), BF16, pltpu.HBM)
    stage = [pltpu.VMEM((width, 2, size, size), BF16), pltpu.SemaphoreType.DMA((width,))]

    def across(array):
        return lax.ppermute(array, "sec", swap)

    sent, edge, env, t0, t1, radius, traces, steps, weights = call(
        functools.partial(first_kernel, width, RUNS[0]),
        "anchor",
        (),
        tuple((a, False) for a in (sources, operators, insert_at, tensors, schmidt)),
        (
            message(RUNS[0]),
            ((2 * HALO, 2 * size, size), BF16, pltpu.VMEM),
            env_shape,
            tensor_shape,
            tensor_shape,
            radius_shape,
            trace_shape,
            ((4,), jnp.int32, pltpu.SMEM),
            ((2, 4), F32, pltpu.SMEM),
        ),
        [pltpu.SMEM(a.shape, a.dtype) for a in (sources, operators, insert_at)] + [pltpu.SemaphoreType.DMA((6,))],
    )
    halo = across(edge)
    got = [lax.ppermute(sent, "site", ring)]
    env, t0, t1, *sents, traces = call(
        functools.partial(second_kernel, width, RUNS[0], RUNS[1:]),
        "anchor_rest",
        (steps, weights),
        ((tensors, False),) + tuple((a, True) for a in (env, halo, t0, t1, radius, traces)),
        (env_shape, tensor_shape, tensor_shape) + (message(RUNS[1]), message(RUNS[2], 0), message(RUNS[3], 0)) + (trace_shape,),
        [pltpu.SemaphoreType.DMA((3,))],
        {3: 0, 5: 1, 6: 2},
    )
    got += [lax.ppermute(s, "site", ring[:-1]) for s in sents]
    env, middle, piece = call(
        functools.partial(open_kernel, width, RUNS[0]),
        "first_run",
        (steps,),
        ((got[0], True),),
        (env_shape, env_shape, message(RUNS[1])),
    )
    ours, env = lax.optimization_barrier((got[1], env))
    final, env, middle, traces, *partials = call(
        functools.partial(edge_kernel, width, RUNS[0][1]),
        "edge",
        (steps,),
        tuple((a, True) for a in (t0, t1, halo, radius, traces, env, middle, ours, across(ours), across(piece))),
        (out_shape, env_shape, env_shape, trace_shape, partial_shape, partial_shape),
        stage,
        {6: 1, 7: 2},
    )
    row = RUNS[1][1] - RUNS[1][0]
    for run, buffer in zip(RUNS[2:], got[2:]):
        if run[1] == width:
            results = (((2, 2, 2), F32, pltpu.VMEM),)
        else:
            begun = 2 * HALO if run[1] + HALO == width else HALO
            results = (((begun, 2 * size, size), F32, pltpu.VMEM), partial_shape)
        final, env, middle, traces, *partials = call(
            functools.partial(next_kernel, width, run, row),
            "run_%d" % run[0],
            (steps,),
            tuple((a, True) for a in (t0, t1, radius, traces, ours, buffer, *partials, env, middle)) + ((final, False),),
            (out_shape, env_shape, env_shape, trace_shape) + results,
            stage,
            {9: 1, 10: 2, 11: 0},
        )
        row += run[1] - run[0]
    (totals,) = partials
    return final, totals + across(totals)


def solution(mesh):
    placed = (
        P(("grp", "site"), None, "sec", None, None),
        P("grp", None, None),
        P(),
        P(("grp", "site"), None),
        P("grp", "sec", None),
    )
    return jax.shard_map(
        shards,
        mesh=mesh,
        in_specs=placed,
        out_specs=(P(("grp", "site"), None, "sec", None, None), P(("grp", "site"), None, None)),
        check_vma=False,
    )
```

```python
import functools

import jax
import jax.numpy as jnp
from jax import lax
from jax.experimental import pallas as pl
from jax.experimental.pallas import tpu as pltpu
from jax.sharding import PartitionSpec as P

F32 = jnp.float32
BF16 = jnp.bfloat16
REACH = 4
HALO = 2
EXTRA = 16
class Place:
    def __init__(self, width, steps):
        self.core = lax.axis_index("sec")
        self.pair = lax.axis_index("site")
        self.width = width
        self.steps = steps

    def local(self, b):
        return jnp.where(self.core == 0, self.width - 1 - b, b)


def dot(a, b):
    return jnp.dot(a, b, preferred_element_type=F32)


def dot_t(a, b):
    return lax.dot_general(a, b, (((0,), (0,)), ((), ())), preferred_element_type=F32)


def diagonal_row(block):
    half = block.shape[0] // 2
    row = lax.broadcasted_iota(jnp.int32, (half, half), 0)
    col = lax.broadcasted_iota(jnp.int32, (half, half), 1)
    parts = [
        jnp.sum(jnp.where(row == col, block[at : at + half, at : at + half], 0.0), axis=0, keepdims=True)
        for at in (0, half)
    ]
    return jnp.concatenate(parts, axis=1)


def pack(first, second):
    half = first.shape[0] // 2
    row = lax.broadcasted_iota(jnp.int32, (half, half), 0)
    col = lax.broadcasted_iota(jnp.int32, (half, half), 1)
    upper = row <= col

    def mixed(at):
        cut = slice(at, at + half)
        return jnp.where(upper, first[cut, cut], second[cut, cut])

    top = jnp.concatenate([mixed(0), first[:half, half:]], axis=1)
    bottom = jnp.concatenate([second[half:, :half], mixed(half)], axis=1)
    return jnp.concatenate([top, bottom], axis=0).astype(BF16)


def unpack(packed, diagonal, valid):
    half = packed.shape[0] // 2
    packed = jnp.where(valid, packed, jnp.zeros_like(packed))
    diagonal = jnp.where(valid, diagonal.astype(F32), 0.0)
    turned = packed.T
    row = lax.broadcasted_iota(jnp.int32, (half, half), 0)
    col = lax.broadcasted_iota(jnp.int32, (half, half), 1)

    def corners(at):
        cut = slice(at, at + half)
        straight, mirrored = packed[cut, cut].astype(F32), turned[cut, cut].astype(F32)
        low = jnp.where(row <= col, straight, mirrored)
        high = jnp.where(row == col, diagonal[:, cut], jnp.where(row < col, mirrored, straight))
        return low.astype(BF16), high.astype(BF16)

    def whole(north, ne, sw, south):
        top = jnp.concatenate([north, ne], axis=1)
        bottom = jnp.concatenate([sw, south], axis=1)
        return jnp.concatenate([top, bottom], axis=0)

    north, south = corners(0), corners(half)
    first = whole(north[0], packed[:half, half:], turned[half:, :half], south[0])
    second = whole(north[1], turned[:half, half:], packed[half:, :half], south[1])
    return first, second


def advance(env, slots, blocks, weight=None):
    size = blocks[0].shape[-1]
    middles = []
    for state in range(2):
        turned = blocks[state].T
        halves = []
        for insert in range(2):
            part = dot(turned, env[slots[state], insert * size : (insert + 1) * size])
            if weight is not None:
                part = part * weight[insert][state]
            halves.append(part.astype(BF16))
        middles.append(jnp.concatenate(halves, axis=0))
    both = dot(jnp.concatenate(middles, axis=1), jnp.concatenate(blocks, axis=0))
    return both[:size], both[size:]


def one_state(place, env, site, state, tensors, b):
    size = env.shape[-1]
    block = tensors[state, place.local(b)]
    slot = REACH + b + place.steps[2 * site + state]
    turned = block.T
    halves = [dot(turned, env[slot, k * size : (k + 1) * size]).astype(BF16) for k in range(2)]
    return dot(jnp.concatenate(halves, axis=0), block)


def early_state(place, site, b, known):
    nearer = 1 - place.core
    return jnp.where(b + place.steps[2 * site + nearer] < known, nearer, 1 - nearer)


def begin(place, todo, known, env, site, tensors, partial):
    for i, b in enumerate(range(*todo)):
        partial[i] = one_state(place, env, site, early_state(place, site, b, known), tensors, b)


def complete(place, i, b, known, env, site, tensors, partial):
    both = partial[i] + one_state(place, env, site, 1 - early_state(place, site, b, known), tensors, b)
    size = env.shape[-1]
    return both[:size], both[size:]


def squares(place, blocks, weight, b):
    terms = [dot(blocks[state].T, blocks[state]) for state in range(2)]
    out = []
    for insert in range(2):
        total = 0.0
        for state in range(2):
            inside = b + place.steps[state] < place.width
            total = total + jnp.where(inside, weight[insert][state], 0.0) * terms[state]
        out.append(total)
    return out


def fill_steps(place, sources, steps):
    middle = sources.shape[2] // 2
    for site in range(2):
        charge = sources[2 * place.pair + site, 0, middle] - middle + 1
        for state in range(2):
            steps[2 * site + state] = (2 * place.core - 1) * (charge + 2 * state - 1)


def fill_weights(operators, insert_at, weights):
    for which in range(2):
        for k in range(2):
            for s in range(2):
                weights[which, 2 * k + s] = jnp.where(insert_at[0, k] == which, operators[k, s], 1.0)


def weights_at(weights, which):
    return [[weights[which, 2 * k + s] for s in range(2)] for k in range(2)]


def add_traces(place, traces, at, site, b, parts, radius):
    row = radius[place.local(b), pl.ds(2 * place.pair + site, 1)]
    for k in range(2):
        traces[at + k : at + k + 1] += diagonal_row(parts[k].astype(BF16).astype(F32)) * (row * row)


def slots_of(place, site, b):
    return [REACH + b + place.steps[2 * site + state] for state in range(2)]


def store_env(env, slot, parts):
    size = parts[0].shape[0]
    for k in range(2):
        env[slot, k * size : (k + 1) * size] = parts[k].astype(BF16)


def blocks_of(place, tensors, b):
    return [tensors[state, place.local(b)] for state in range(2)]


def send(place, env, t1, weight, traces, radius, sent, run):
    rows = []
    for b in range(*run):
        parts = advance(env, slots_of(place, 1, b), blocks_of(place, t1, b), weight)
        size = parts[0].shape[0]
        sent[(b - run[0]) * size : (b - run[0] + 1) * size] = pack(*parts)
        add_traces(place, traces, 4, 1, b, parts, radius)
        rows.append(diagonal_row(parts[1]))
    return rows


def send_rows(sent, rows):
    rows = jnp.concatenate(rows, axis=0)
    rows = jnp.concatenate([rows, jnp.zeros((EXTRA - rows.shape[0], rows.shape[1]), F32)], axis=0)
    sent[sent.shape[0] - EXTRA :] = rows.astype(BF16)


def below(buffer):
    return buffer[buffer.shape[0] - EXTRA :]


def take(place, buffer, i, diagonals, row, env, slot):
    size = buffer.shape[1]
    store_env(env, slot, unpack(buffer[i * size : (i + 1) * size], diagonals[row : row + 1], place.pair > 0))


class Loads:
    def __init__(self):
        self.waiting = {}

    def start(self, key, source, target, sem):
        copy = pltpu.make_async_copy(source, target, sem)
        copy.start()
        self.waiting[key] = copy

    def tensors(self, place, source, target, site, lo, hi, sem):
        at = pl.ds(jnp.where(place.core == 0, place.width - hi, lo), hi - lo)
        self.start((site, lo), source.at[site, :, at], target.at[:, at], sem)

    def wait(self, *keys):
        for key in keys:
            if key in self.waiting:
                self.waiting.pop(key).wait()


def first_kernel(width, run, sources, operators, insert_at, tensors, schmidt,
                 sent, edge, env, t0, t1, radius, traces, steps, weights, sources_here, operators_here, inserts_here, sems):
    place = Place(width, steps)
    lo, hi = run
    loads = Loads()
    loads.start("sources", sources, sources_here, sems.at[0])
    loads.start("operators", operators, operators_here, sems.at[1])
    loads.start("insert_at", insert_at, inserts_here, sems.at[2])
    near = hi + HALO
    loads.tensors(place, tensors, t0, 0, 0, near, sems.at[3])
    loads.tensors(place, tensors, t1, 1, lo, hi, sems.at[4])
    loads.start("radius", schmidt, radius, sems.at[5])
    traces[...] = jnp.zeros_like(traces)
    env[REACH + width :] = jnp.zeros_like(env[REACH + width :])
    loads.wait("sources", "operators", "insert_at")
    fill_steps(place, sources_here, steps)
    fill_weights(operators_here, inserts_here, weights)
    u, v = weights_at(weights, 0), weights_at(weights, 1)
    loads.wait((0, 0))
    for b in range(near):
        blocks = blocks_of(place, t0, b)
        parts = squares(place, blocks, u, b)
        store_env(env, REACH + b, parts)
        if b < HALO:
            store_env(edge, HALO - 1 - b, parts)
            edge[2 * HALO - 1 - b] = jnp.concatenate(blocks, axis=0)
    loads.wait((1, lo), "radius")
    send_rows(sent, send(place, env, t1, v, traces, radius, sent, run))


def second_kernel(width, first_run, runs, steps, weights, tensors, old_env, halo, old_t0, old_t1, radius,
                  old_traces, *rest):
    env, t0, t1, sents, (traces, sems) = *rest[:3], rest[3:-2], rest[-2:]
    place = Place(width, steps)
    size = t0.shape[-1]
    lo, hi = first_run
    known = hi + HALO
    loads = Loads()
    loads.tensors(place, tensors, t0, 0, known, width, sems.at[0])
    loads.tensors(place, tensors, t1, 1, hi, width, sems.at[1])
    loads.tensors(place, tensors, t1, 1, 0, lo, sems.at[2])
    u, v = weights_at(weights, 0), weights_at(weights, 1)
    traces[...] = old_traces[...]
    for i in range(HALO):
        env[REACH - HALO + i] = halo[i]
    for b in range(known):
        parts = [env[REACH + b, k * size : (k + 1) * size] for k in range(2)]
        add_traces(place, traces, 0, 0, b, parts, radius)
    loads.wait((0, known))
    for b in range(known, width):
        parts = squares(place, blocks_of(place, t0, b), u, b)
        store_env(env, REACH + b, parts)
        add_traces(place, traces, 0, 0, b, parts, radius)
    loads.wait((1, hi), (1, 0))
    rows = []
    for run, sent in zip(runs, sents):
        rows += send(place, env, t1, v, traces, radius, sent, run)
    send_rows(sents[0], rows)


def middle_blocks(place, todo, env, middle, t0, traces, radius, partial=None, known=0):
    for i, b in enumerate(range(*todo)):
        if partial is not None and i < partial.shape[0]:
            parts = complete(place, i, b, known, env, 0, t0, partial)
        else:
            parts = advance(env, slots_of(place, 0, b), blocks_of(place, t0, b))
        store_env(middle, REACH + b, parts)
        add_traces(place, traces, 2, 0, b, parts, radius)


def open_kernel(width, run, steps, first, env, middle, piece):
    place = Place(width, steps)
    size = first.shape[1]
    for array in (env, middle):
        array[REACH + width :] = jnp.zeros_like(array[REACH + width :])
    lo, hi = run
    for b in range(lo, hi):
        take(place, first, b - lo, below(first), b - lo, env, REACH + b)
    piece[: HALO * size] = first[: HALO * size]
    piece[HALO * size :] = below(first)


def final_blocks(place, todo, middle, t1, traces, radius, stage, out, sems, partial=None, known=0):
    stores = Loads()
    for i, b in enumerate(range(*todo)):
        if partial is not None and i < partial.shape[0]:
            parts = complete(place, i, b, known, middle, 1, t1, partial)
        else:
            parts = advance(middle, slots_of(place, 1, b), blocks_of(place, t1, b))
        for k in range(2):
            stage[b, k] = parts[k].astype(BF16)
        if out is not None:
            stores.start(b, stage.at[b], out.at[0, :, place.local(b)], sems.at[b])
        add_traces(place, traces, 6, 1, b, parts, radius)
    return stores


def edge_kernel(width, known, steps, t0, t1, halo, radius, old_traces, old_env, old_middle, ours, near, far,
                out, env, middle, traces, partial0, partial1, stage, sems):
    place = Place(width, steps)
    size = t0.shape[-1]
    traces[...] = old_traces[...]
    for i in range(HALO):
        take(place, ours, i, below(ours), i, env, REACH + i)
        take(place, near, i, below(near), i, env, REACH - 1 - i)
        take(place, far, i, below(far), i, env, REACH - 1 - HALO - i)
    for i in range(HALO):
        blocks = [halo[HALO + i, state * size : (state + 1) * size] for state in range(2)]
        store_env(middle, REACH - HALO + i, advance(env, slots_of(place, 0, i - HALO), blocks))
    middle_blocks(place, (0, known - HALO), env, middle, t0, traces, radius)
    last = (0, known - 2 * HALO)
    stores = final_blocks(place, last, middle, t1, traces, radius, stage, out, sems)
    begin(place, (known - HALO, known), known, env, 0, t0, partial0)
    begin(place, (last[1], last[1] + HALO), known - HALO, middle, 1, t1, partial1)
    stores.wait(*range(*last))


def next_kernel(width, run, row, steps, t0, t1, radius, old_traces, ours, buffer, old_partial0, old_partial1, old_env, old_middle,
                *rest):
    lo, hi = run
    if hi == width:
        env, middle, traces, totals, stage = rest
        out = sems = None
    else:
        out, env, middle, traces, *results, stage, sems = rest[1:]
    place = Place(width, steps)
    for b in range(lo, hi):
        take(place, buffer, b - lo, below(ours), row + b - lo, env, REACH + b)
    traces[...] = old_traces[...]
    ends = hi == width
    upto = width if ends else hi - HALO
    middle_blocks(place, (lo - HALO, upto), env, middle, t0, traces, radius, old_partial0, lo)
    last = (lo - 2 * HALO, width if ends else upto - HALO)
    stores = final_blocks(place, last, middle, t1, traces, radius, stage, out, sems, old_partial1, lo - HALO)
    if ends:
        totals[...] = jnp.zeros_like(totals)
        sums = jnp.sum(traces[...], axis=1, keepdims=True)
        for j in range(2):
            for t in range(2):
                at = 4 * j + 2 * t
                totals[j, t : t + 1, :2] = jnp.concatenate([sums[at : at + 1], sums[at + 1 : at + 2]], axis=1)
    else:
        begin(place, (upto, upto + results[0].shape[0]), hi, env, 0, t0, results[0])
        begin(place, (last[1], upto), upto, middle, 1, t1, results[1])
    if out is not None:
        stores.wait(*range(*last))


def store_kernel(width, todo, steps, stage, old_out, out, sems):
    place = Place(width, steps)
    stores = Loads()
    for b in range(*todo):
        stores.start(b, stage.at[b], out.at[0, :, place.local(b)], sems.at[b])
    stores.wait(*range(*todo))


SMEM = pl.BlockSpec(memory_space=pltpu.SMEM)
VMEM = pl.BlockSpec(memory_space=pltpu.VMEM)
HBM = pl.BlockSpec(memory_space=pl.ANY)
PARAMS = pltpu.CompilerParams(vmem_limit_bytes=28 * 2**20)
RUNS = ((2, 5), (0, 2), (5, 8), (8, 10))


def call(kernel, name, scalars, arrays, outs, scratch=(), aliases=None):
    specs = {pltpu.VMEM: VMEM, pltpu.SMEM: SMEM, pltpu.HBM: HBM}
    where = [pltpu.SMEM] * len(scalars) + [pltpu.VMEM if near else pltpu.HBM for _, near in arrays]
    values = [*scalars, *[a for a, _ in arrays]]
    return pl.pallas_call(
        kernel,
        out_shape=tuple(memory(s, d) for s, d, memory in outs),
        in_specs=[specs[w] for w in where],
        out_specs=tuple(specs[memory] for _, _, memory in outs),
        scratch_shapes=list(scratch),
        compiler_params=PARAMS,
        input_output_aliases={} if aliases is None else aliases,
        name=name,
    )(*[pltpu.with_memory_space_constraint(a, w) for a, w in zip(values, where)])


def shards(tensors, sources, operators, insert_at, schmidt):
    width, size = tensors.shape[2], tensors.shape[-1]
    pairs = lax.axis_size("site")
    ring = [(i, (i + 1) % pairs) for i in range(pairs)]
    swap = [(0, 1), (1, 0)]
    schmidt = jnp.swapaxes(schmidt, 0, 1)

    def message(run, extra=EXTRA):
        return ((run[1] - run[0]) * size + extra, size), BF16, pltpu.VMEM

    trace_shape = ((8, size), F32, pltpu.VMEM)
    env_shape = ((width + REACH + HALO, 2 * size, size), BF16, pltpu.VMEM)
    tensor_shape = ((2, width, size, size), BF16, pltpu.VMEM)
    partial_shape = ((HALO, 2 * size, size), F32, pltpu.VMEM)
    radius_shape = (schmidt.shape, F32, pltpu.VMEM)
    out_shape = ((1, 2, width, size, size), BF16, pltpu.HBM)
    stage = [pltpu.VMEM((width, 2, size, size), BF16), pltpu.SemaphoreType.DMA((width,))]

    def across(array):
        return lax.ppermute(array, "sec", swap)

    sent, edge, env, t0, t1, radius, traces, steps, weights = call(
        functools.partial(first_kernel, width, RUNS[0]),
        "anchor",
        (),
        tuple((a, False) for a in (sources, operators, insert_at, tensors, schmidt)),
        (
            message(RUNS[0]),
            ((2 * HALO, 2 * size, size), BF16, pltpu.VMEM),
            env_shape,
            tensor_shape,
            tensor_shape,
            radius_shape,
            trace_shape,
            ((4,), jnp.int32, pltpu.SMEM),
            ((2, 4), F32, pltpu.SMEM),
        ),
        [pltpu.SMEM(a.shape, a.dtype) for a in (sources, operators, insert_at)] + [pltpu.SemaphoreType.DMA((6,))],
    )
    halo = across(edge)
    got = [lax.ppermute(sent, "site", ring)]
    env, t0, t1, *sents, traces = call(
        functools.partial(second_kernel, width, RUNS[0], RUNS[1:]),
        "anchor_rest",
        (steps, weights),
        ((tensors, False),) + tuple((a, True) for a in (env, halo, t0, t1, radius, traces)),
        (env_shape, tensor_shape, tensor_shape) + (message(RUNS[1]), message(RUNS[2], 0), message(RUNS[3], 0)) + (trace_shape,),
        [pltpu.SemaphoreType.DMA((3,))],
        {3: 0, 5: 1, 6: 2},
    )
    got += [lax.ppermute(s, "site", ring[:-1]) for s in sents]
    env, middle, piece = call(
        functools.partial(open_kernel, width, RUNS[0]),
        "first_run",
        (steps,),
        ((got[0], True),),
        (env_shape, env_shape, message(RUNS[1])),
    )
    ours, env = lax.optimization_barrier((got[1], env))
    final, env, middle, traces, *partials = call(
        functools.partial(edge_kernel, width, RUNS[0][1]),
        "edge",
        (steps,),
        tuple((a, True) for a in (t0, t1, halo, radius, traces, env, middle, ours, across(ours), across(piece))),
        (out_shape, env_shape, env_shape, trace_shape, partial_shape, partial_shape),
        stage,
        {6: 1, 7: 2},
    )
    row = RUNS[1][1] - RUNS[1][0]
    run, last = RUNS[2:]
    final, env, middle, traces, *partials = call(
        functools.partial(next_kernel, width, run, row),
        "third_run",
        (steps,),
        tuple((a, True) for a in (t0, t1, radius, traces, ours, got[2], *partials, env, middle)) + ((final, False),),
        (out_shape, env_shape, env_shape, trace_shape, ((2 * HALO, 2 * size, size), F32, pltpu.VMEM), partial_shape),
        stage,
        {9: 1, 10: 2, 11: 0},
    )
    env, middle, traces, totals, blocks = call(
        functools.partial(next_kernel, width, last, row + run[1] - run[0]),
        "last_run",
        (steps,),
        tuple((a, True) for a in (t0, t1, radius, traces, ours, got[3], *partials, env, middle)),
        (env_shape, env_shape, trace_shape, ((2, 16, 128), F32, pltpu.VMEM), ((width, 2, size, size), BF16, pltpu.VMEM)),
        aliases={9: 0, 10: 1},
    )
    others = across(totals)
    (final,) = call(
        functools.partial(store_kernel, width, (last[0] - 2 * HALO, width)),
        "store",
        (steps,),
        ((blocks, True), (final, False)),
        (out_shape,),
        stage[1:],
        {2: 0},
    )
    return final, totals[:, :2, :2] + others[:, :2, :2]


def solution(mesh):
    placed = (
        P(("grp", "site"), None, "sec", None, None),
        P("grp", None, None),
        P(),
        P(("grp", "site"), None),
        P("grp", "sec", None),
    )
    return jax.shard_map(
        shards,
        mesh=mesh,
        in_specs=placed,
        out_specs=(P(("grp", "site"), None, "sec", None, None), P(("grp", "site"), None, None)),
        check_vma=False,
    )
```

```python
import functools

import jax
import jax.numpy as jnp
from jax import lax
from jax.experimental import pallas as pl
from jax.experimental.pallas import tpu as pltpu
from jax.sharding import PartitionSpec as P

F32 = jnp.float32
BF16 = jnp.bfloat16
REACH = 4
HALO = 2
EXTRA = 16
class Place:
    def __init__(self, width, steps):
        self.core = lax.axis_index("sec")
        self.pair = lax.axis_index("site")
        self.width = width
        self.steps = steps

    def local(self, b):
        return jnp.where(self.core == 0, self.width - 1 - b, b)


def dot(a, b):
    return jnp.dot(a, b, preferred_element_type=F32)


def dot_t(a, b):
    return lax.dot_general(a, b, (((0,), (0,)), ((), ())), preferred_element_type=F32)


def diagonal_row(block):
    half = block.shape[0] // 2
    row = lax.broadcasted_iota(jnp.int32, (half, half), 0)
    col = lax.broadcasted_iota(jnp.int32, (half, half), 1)
    parts = [
        jnp.sum(jnp.where(row == col, block[at : at + half, at : at + half], 0.0), axis=0, keepdims=True)
        for at in (0, half)
    ]
    return jnp.concatenate(parts, axis=1)


def pack(first, second):
    half = first.shape[0] // 2
    row = lax.broadcasted_iota(jnp.int32, (half, half), 0)
    col = lax.broadcasted_iota(jnp.int32, (half, half), 1)
    upper = row <= col

    def mixed(at):
        cut = slice(at, at + half)
        return jnp.where(upper, first[cut, cut], second[cut, cut])

    top = jnp.concatenate([mixed(0), first[:half, half:]], axis=1)
    bottom = jnp.concatenate([second[half:, :half], mixed(half)], axis=1)
    return jnp.concatenate([top, bottom], axis=0).astype(BF16)


def unpack(packed, diagonal, valid):
    half = packed.shape[0] // 2
    packed = jnp.where(valid, packed, jnp.zeros_like(packed))
    diagonal = jnp.where(valid, diagonal.astype(F32), 0.0)
    turned = packed.T
    row = lax.broadcasted_iota(jnp.int32, (half, half), 0)
    col = lax.broadcasted_iota(jnp.int32, (half, half), 1)

    def corners(at):
        cut = slice(at, at + half)
        straight, mirrored = packed[cut, cut].astype(F32), turned[cut, cut].astype(F32)
        low = jnp.where(row <= col, straight, mirrored)
        high = jnp.where(row == col, diagonal[:, cut], jnp.where(row < col, mirrored, straight))
        return low.astype(BF16), high.astype(BF16)

    def whole(north, ne, sw, south):
        top = jnp.concatenate([north, ne], axis=1)
        bottom = jnp.concatenate([sw, south], axis=1)
        return jnp.concatenate([top, bottom], axis=0)

    north, south = corners(0), corners(half)
    first = whole(north[0], packed[:half, half:], turned[half:, :half], south[0])
    second = whole(north[1], turned[:half, half:], packed[half:, :half], south[1])
    return first, second


def advance(env, slots, blocks, weight=None):
    size = blocks[0].shape[-1]
    middles = []
    for state in range(2):
        turned = blocks[state].T
        halves = []
        for insert in range(2):
            part = dot(turned, env[slots[state], insert * size : (insert + 1) * size])
            if weight is not None:
                part = part * weight[insert][state]
            halves.append(part.astype(BF16))
        middles.append(jnp.concatenate(halves, axis=0))
    both = dot(jnp.concatenate(middles, axis=1), jnp.concatenate(blocks, axis=0))
    return both[:size], both[size:]


def one_state(place, env, site, state, tensors, b):
    size = env.shape[-1]
    block = tensors[state, place.local(b)]
    slot = REACH + b + place.steps[2 * site + state]
    turned = block.T
    halves = [dot(turned, env[slot, k * size : (k + 1) * size]).astype(BF16) for k in range(2)]
    return dot(jnp.concatenate(halves, axis=0), block)


def early_state(place, site, b, known):
    nearer = 1 - place.core
    return jnp.where(b + place.steps[2 * site + nearer] < known, nearer, 1 - nearer)


def begin(place, todo, known, env, site, tensors, partial):
    for i, b in enumerate(range(*todo)):
        partial[i] = one_state(place, env, site, early_state(place, site, b, known), tensors, b)


def complete(place, i, b, known, env, site, tensors, partial):
    both = partial[i] + one_state(place, env, site, 1 - early_state(place, site, b, known), tensors, b)
    size = env.shape[-1]
    return both[:size], both[size:]


def squares(place, blocks, weight, b):
    terms = [dot(blocks[state].T, blocks[state]) for state in range(2)]
    out = []
    for insert in range(2):
        total = 0.0
        for state in range(2):
            inside = b + place.steps[state] < place.width
            total = total + jnp.where(inside, weight[insert][state], 0.0) * terms[state]
        out.append(total)
    return out


def fill_steps(place, sources, steps):
    middle = sources.shape[2] // 2
    for site in range(2):
        charge = sources[2 * place.pair + site, 0, middle] - middle + 1
        for state in range(2):
            steps[2 * site + state] = (2 * place.core - 1) * (charge + 2 * state - 1)


def fill_weights(operators, insert_at, weights):
    for which in range(2):
        for k in range(2):
            for s in range(2):
                weights[which, 2 * k + s] = jnp.where(insert_at[0, k] == which, operators[k, s], 1.0)


def weights_at(weights, which):
    return [[weights[which, 2 * k + s] for s in range(2)] for k in range(2)]


def add_traces(place, traces, at, site, b, parts, radius):
    row = radius[place.local(b), pl.ds(2 * place.pair + site, 1)]
    for k in range(2):
        traces[at + k : at + k + 1] += diagonal_row(parts[k].astype(BF16).astype(F32)) * (row * row)


def slots_of(place, site, b):
    return [REACH + b + place.steps[2 * site + state] for state in range(2)]


def store_env(env, slot, parts):
    size = parts[0].shape[0]
    for k in range(2):
        env[slot, k * size : (k + 1) * size] = parts[k].astype(BF16)


def blocks_of(place, tensors, b):
    return [tensors[state, place.local(b)] for state in range(2)]


def send(place, env, t1, weight, traces, radius, sent, run):
    rows = []
    for b in range(*run):
        parts = advance(env, slots_of(place, 1, b), blocks_of(place, t1, b), weight)
        size = parts[0].shape[0]
        sent[(b - run[0]) * size : (b - run[0] + 1) * size] = pack(*parts)
        add_traces(place, traces, 4, 1, b, parts, radius)
        rows.append(diagonal_row(parts[1]))
    return rows


def send_rows(sent, rows):
    rows = jnp.concatenate(rows, axis=0)
    rows = jnp.concatenate([rows, jnp.zeros((EXTRA - rows.shape[0], rows.shape[1]), F32)], axis=0)
    sent[sent.shape[0] - EXTRA :] = rows.astype(BF16)


def below(buffer):
    return buffer[buffer.shape[0] - EXTRA :]


def take(place, buffer, i, diagonals, row, env, slot):
    size = buffer.shape[1]
    store_env(env, slot, unpack(buffer[i * size : (i + 1) * size], diagonals[row : row + 1], place.pair > 0))


class Loads:
    def __init__(self):
        self.waiting = {}

    def start(self, key, source, target, sem):
        copy = pltpu.make_async_copy(source, target, sem)
        copy.start()
        self.waiting[key] = copy

    def tensors(self, place, source, target, site, lo, hi, sem):
        at = pl.ds(jnp.where(place.core == 0, place.width - hi, lo), hi - lo)
        for state in range(2):
            self.start((site, lo, state), source.at[site, state, at], target.at[state, at], sem.at[state])

    def wait(self, *keys):
        for key in keys:
            if key in self.waiting:
                self.waiting.pop(key).wait()


def first_kernel(width, run, sources, operators, insert_at, tensors, schmidt,
                 sent, edge, env, t0, t1, radius, traces, rows, steps, weights, sources_here, operators_here, inserts_here, sems):
    place = Place(width, steps)
    lo, hi = run
    loads = Loads()
    loads.start("sources", sources, sources_here, sems.at[0])
    loads.start("operators", operators, operators_here, sems.at[1])
    loads.start("insert_at", insert_at, inserts_here, sems.at[2])
    near = hi + HALO
    loads.tensors(place, tensors, t0, 0, 0, near, sems.at[pl.ds(3, 2)])
    loads.tensors(place, tensors, t1, 1, lo, hi, sems.at[pl.ds(5, 2)])
    loads.start("radius", schmidt, radius, sems.at[7])
    traces[...] = jnp.zeros_like(traces)
    env[REACH + width :] = jnp.zeros_like(env[REACH + width :])
    loads.wait("sources", "operators", "insert_at")
    fill_steps(place, sources_here, steps)
    fill_weights(operators_here, inserts_here, weights)
    u, v = weights_at(weights, 0), weights_at(weights, 1)
    loads.wait((0, 0, 0), (0, 0, 1))
    for b in range(near):
        blocks = blocks_of(place, t0, b)
        parts = squares(place, blocks, u, b)
        store_env(env, REACH + b, parts)
        if b < HALO:
            store_env(edge, HALO - 1 - b, parts)
            edge[2 * HALO - 1 - b] = jnp.concatenate(blocks, axis=0)
    loads.wait((1, lo, 0), (1, lo, 1), "radius")
    send_rows(rows, send(place, env, t1, v, traces, radius, sent, run))


def second_kernel(width, first_run, runs, steps, weights, tensors, old_env, halo, old_t0, old_t1, radius,
                  old_traces, first_rows, *rest):
    env, t0, t1, sents, (traces, sems) = *rest[:3], rest[3:-2], rest[-2:]
    place = Place(width, steps)
    size = t0.shape[-1]
    lo, hi = first_run
    known = hi + HALO
    loads = Loads()
    loads.tensors(place, tensors, t0, 0, known, width, sems.at[pl.ds(0, 2)])
    loads.tensors(place, tensors, t1, 1, hi, width, sems.at[pl.ds(2, 2)])
    loads.tensors(place, tensors, t1, 1, 0, lo, sems.at[pl.ds(4, 2)])
    u, v = weights_at(weights, 0), weights_at(weights, 1)
    traces[...] = old_traces[...]
    for i in range(HALO):
        env[REACH - HALO + i] = halo[i]
    for b in range(known):
        parts = [env[REACH + b, k * size : (k + 1) * size] for k in range(2)]
        add_traces(place, traces, 0, 0, b, parts, radius)
    loads.wait((0, known, 0), (0, known, 1))
    for b in range(known, width):
        parts = squares(place, blocks_of(place, t0, b), u, b)
        store_env(env, REACH + b, parts)
        add_traces(place, traces, 0, 0, b, parts, radius)
    loads.wait((1, hi, 0), (1, hi, 1), (1, 0, 0), (1, 0, 1))
    rows = []
    for run, sent in zip(runs, sents):
        rows += send(place, env, t1, v, traces, radius, sent, run)
    send_rows(sents[0], rows + [first_rows[: hi - lo].astype(F32)])


def middle_blocks(place, todo, env, middle, t0, traces, radius, partial=None, known=0):
    for i, b in enumerate(range(*todo)):
        if partial is not None and i < partial.shape[0]:
            parts = complete(place, i, b, known, env, 0, t0, partial)
        else:
            parts = advance(env, slots_of(place, 0, b), blocks_of(place, t0, b))
        store_env(middle, REACH + b, parts)
        add_traces(place, traces, 2, 0, b, parts, radius)


def open_kernel(steps, first, env, middle, piece, width):
    for array in (env, middle):
        array[REACH + width :] = jnp.zeros_like(array[REACH + width :])
    piece[...] = first[: piece.shape[0]]


def final_blocks(place, todo, middle, t1, traces, radius, stage, out, sems, partial=None, known=0):
    stores = Loads()
    for i, b in enumerate(range(*todo)):
        if partial is not None and i < partial.shape[0]:
            parts = complete(place, i, b, known, middle, 1, t1, partial)
        else:
            parts = advance(middle, slots_of(place, 1, b), blocks_of(place, t1, b))
        for k in range(2):
            stage[b, k] = parts[k].astype(BF16)
        if out is not None:
            stores.start(b, stage.at[b], out.at[0, :, place.local(b)], sems.at[b])
        add_traces(place, traces, 6, 1, b, parts, radius)
    return stores


def edge_kernel(width, run, steps, t0, t1, halo, radius, old_traces, old_env, old_middle, first, ours, near, far,
                out, env, middle, traces, partial0, partial1, stage, sems):
    place = Place(width, steps)
    lo, known = run
    size = t0.shape[-1]
    traces[...] = old_traces[...]
    for i in range(HALO):
        take(place, ours, i, below(ours), i, env, REACH + i)
        take(place, near, i, below(near), i, env, REACH - 1 - i)
        take(place, far, i, below(near), width - (known - lo) + i, env, REACH - 1 - HALO - i)
    for b in range(lo, known):
        take(place, first, b - lo, below(ours), width - known + b, env, REACH + b)
    for i in range(HALO):
        blocks = [halo[HALO + i, state * size : (state + 1) * size] for state in range(2)]
        store_env(middle, REACH - HALO + i, advance(env, slots_of(place, 0, i - HALO), blocks))
    middle_blocks(place, (0, known - HALO), env, middle, t0, traces, radius)
    last = (0, known - 2 * HALO)
    stores = final_blocks(place, last, middle, t1, traces, radius, stage, out, sems)
    begin(place, (known - HALO, known), known, env, 0, t0, partial0)
    begin(place, (last[1], last[1] + HALO), known - HALO, middle, 1, t1, partial1)
    stores.wait(*range(*last))


def next_kernel(width, run, row, steps, t0, t1, radius, old_traces, ours, buffer, old_partial0, old_partial1, old_env, old_middle,
                *rest):
    lo, hi = run
    if hi == width:
        env, middle, traces, totals, stage = rest
        out = sems = None
    else:
        out, env, middle, traces, *results, stage, sems = rest[1:]
    place = Place(width, steps)
    for b in range(lo, hi):
        take(place, buffer, b - lo, below(ours), row + b - lo, env, REACH + b)
    traces[...] = old_traces[...]
    ends = hi == width
    upto = width if ends else hi - HALO
    middle_blocks(place, (lo - HALO, upto), env, middle, t0, traces, radius, old_partial0, lo)
    last = (lo - 2 * HALO, width if ends else upto - HALO)
    stores = final_blocks(place, last, middle, t1, traces, radius, stage, out, sems, old_partial1, lo - HALO)
    if ends:
        totals[...] = jnp.zeros_like(totals)
        sums = jnp.sum(traces[...], axis=1, keepdims=True)
        for j in range(2):
            for t in range(2):
                at = 4 * j + 2 * t
                totals[j, t : t + 1, :2] = jnp.concatenate([sums[at : at + 1], sums[at + 1 : at + 2]], axis=1)
    else:
        begin(place, (upto, upto + results[0].shape[0]), hi, env, 0, t0, results[0])
        begin(place, (last[1], upto), upto, middle, 1, t1, results[1])
    if out is not None:
        stores.wait(*range(*last))


def store_kernel(width, todo, steps, stage, old_out, out, sems):
    place = Place(width, steps)
    stores = Loads()
    for b in range(*todo):
        stores.start(b, stage.at[b], out.at[0, :, place.local(b)], sems.at[b])
    stores.wait(*range(*todo))


SMEM = pl.BlockSpec(memory_space=pltpu.SMEM)
VMEM = pl.BlockSpec(memory_space=pltpu.VMEM)
HBM = pl.BlockSpec(memory_space=pl.ANY)
PARAMS = pltpu.CompilerParams(vmem_limit_bytes=28 * 2**20)
RUNS = ((2, 5), (0, 2), (5, 8), (8, 10))


def call(kernel, name, scalars, arrays, outs, scratch=(), aliases=None):
    specs = {pltpu.VMEM: VMEM, pltpu.SMEM: SMEM, pltpu.HBM: HBM}
    where = [pltpu.SMEM] * len(scalars) + [pltpu.VMEM if near else pltpu.HBM for _, near in arrays]
    values = [*scalars, *[a for a, _ in arrays]]
    return pl.pallas_call(
        kernel,
        out_shape=tuple(memory(s, d) for s, d, memory in outs),
        in_specs=[specs[w] for w in where],
        out_specs=tuple(specs[memory] for _, _, memory in outs),
        scratch_shapes=list(scratch),
        compiler_params=PARAMS,
        input_output_aliases={} if aliases is None else aliases,
        name=name,
    )(*[pltpu.with_memory_space_constraint(a, w) for a, w in zip(values, where)])


def shards(tensors, sources, operators, insert_at, schmidt):
    width, size = tensors.shape[2], tensors.shape[-1]
    pairs = lax.axis_size("site")
    ring = [(i, (i + 1) % pairs) for i in range(pairs)]
    swap = [(0, 1), (1, 0)]
    schmidt = jnp.swapaxes(schmidt, 0, 1)

    def message(run, extra=EXTRA):
        return ((run[1] - run[0]) * size + extra, size), BF16, pltpu.VMEM

    trace_shape = ((8, size), F32, pltpu.VMEM)
    env_shape = ((width + REACH + HALO, 2 * size, size), BF16, pltpu.VMEM)
    tensor_shape = ((2, width, size, size), BF16, pltpu.VMEM)
    partial_shape = ((HALO, 2 * size, size), F32, pltpu.VMEM)
    radius_shape = (schmidt.shape, F32, pltpu.VMEM)
    out_shape = ((1, 2, width, size, size), BF16, pltpu.HBM)
    stage = [pltpu.VMEM((width, 2, size, size), BF16), pltpu.SemaphoreType.DMA((width,))]

    def across(array):
        return lax.ppermute(array, "sec", swap)

    sent, edge, env, t0, t1, radius, traces, rows, steps, weights = call(
        functools.partial(first_kernel, width, RUNS[0]),
        "anchor",
        (),
        tuple((a, False) for a in (sources, operators, insert_at, tensors, schmidt)),
        (
            message(RUNS[0], 0),
            ((2 * HALO, 2 * size, size), BF16, pltpu.VMEM),
            env_shape,
            tensor_shape,
            tensor_shape,
            radius_shape,
            trace_shape,
            ((EXTRA, size), BF16, pltpu.VMEM),
            ((4,), jnp.int32, pltpu.SMEM),
            ((2, 4), F32, pltpu.SMEM),
        ),
        [pltpu.SMEM(a.shape, a.dtype) for a in (sources, operators, insert_at)] + [pltpu.SemaphoreType.DMA((8,))],
    )
    halo = across(edge)
    got = [lax.ppermute(sent, "site", ring)]
    env, t0, t1, *sents, traces = call(
        functools.partial(second_kernel, width, RUNS[0], RUNS[1:]),
        "anchor_rest",
        (steps, weights),
        ((tensors, False),) + tuple((a, True) for a in (env, halo, t0, t1, radius, traces, rows)),
        (env_shape, tensor_shape, tensor_shape) + (message(RUNS[1]), message(RUNS[2], 0), message(RUNS[3], 0)) + (trace_shape,),
        [pltpu.SemaphoreType.DMA((6,))],
        {3: 0, 5: 1, 6: 2},
    )
    got += [lax.ppermute(s, "site", ring[:-1]) for s in sents]
    env, middle, piece = call(
        functools.partial(open_kernel, width=width),
        "first_run",
        (steps,),
        ((got[0], True),),
        (env_shape, env_shape, message(RUNS[1], 0)),
    )
    ours, env = lax.optimization_barrier((got[1], env))
    final, env, middle, traces, *partials = call(
        functools.partial(edge_kernel, width, RUNS[0]),
        "edge",
        (steps,),
        tuple((a, True) for a in (t0, t1, halo, radius, traces, env, middle, got[0], ours, across(ours), across(piece))),
        (out_shape, env_shape, env_shape, trace_shape, partial_shape, partial_shape),
        stage,
        {6: 1, 7: 2},
    )
    row = RUNS[1][1] - RUNS[1][0]
    run, last = RUNS[2:]
    final, env, middle, traces, *partials = call(
        functools.partial(next_kernel, width, run, row),
        "third_run",
        (steps,),
        tuple((a, True) for a in (t0, t1, radius, traces, ours, got[2], *partials, env, middle)) + ((final, False),),
        (out_shape, env_shape, env_shape, trace_shape, ((2 * HALO, 2 * size, size), F32, pltpu.VMEM), partial_shape),
        stage,
        {9: 1, 10: 2, 11: 0},
    )
    env, middle, traces, totals, blocks = call(
        functools.partial(next_kernel, width, last, row + run[1] - run[0]),
        "last_run",
        (steps,),
        tuple((a, True) for a in (t0, t1, radius, traces, ours, got[3], *partials, env, middle)),
        (env_shape, env_shape, trace_shape, ((2, 16, 128), F32, pltpu.VMEM), ((width, 2, size, size), BF16, pltpu.VMEM)),
        aliases={9: 0, 10: 1},
    )
    others = across(totals)
    (final,) = call(
        functools.partial(store_kernel, width, (last[0] - 2 * HALO, width)),
        "store",
        (steps,),
        ((blocks, True), (final, False)),
        (out_shape,),
        stage[1:],
        {2: 0},
    )
    return final, totals[:, :2, :2] + others[:, :2, :2]


def solution(mesh):
    placed = (
        P(("grp", "site"), None, "sec", None, None),
        P("grp", None, None),
        P(),
        P(("grp", "site"), None),
        P("grp", "sec", None),
    )
    return jax.shard_map(
        shards,
        mesh=mesh,
        in_specs=placed,
        out_specs=(P(("grp", "site"), None, "sec", None, None), P(("grp", "site"), None, None)),
        check_vma=False,
    )
```

```python
import functools

import jax
import jax.numpy as jnp
from jax import lax
from jax.experimental import pallas as pl
from jax.experimental.pallas import tpu as pltpu
from jax.sharding import PartitionSpec as P

F32 = jnp.float32
BF16 = jnp.bfloat16
REACH = 4
HALO = 2
EXTRA = 16
class Place:
    def __init__(self, width, steps):
        self.core = lax.axis_index("sec")
        self.pair = lax.axis_index("site")
        self.width = width
        self.steps = steps

    def local(self, b):
        return jnp.where(self.core == 0, self.width - 1 - b, b)


def dot(a, b):
    return jnp.dot(a, b, preferred_element_type=F32)


def dot_t(a, b):
    return lax.dot_general(a, b, (((0,), (0,)), ((), ())), preferred_element_type=F32)


def diagonal_row(block):
    half = block.shape[0] // 2
    row = lax.broadcasted_iota(jnp.int32, (half, half), 0)
    col = lax.broadcasted_iota(jnp.int32, (half, half), 1)
    parts = [
        jnp.sum(jnp.where(row == col, block[at : at + half, at : at + half], 0.0), axis=0, keepdims=True)
        for at in (0, half)
    ]
    return jnp.concatenate(parts, axis=1)


def pack(first, second):
    half = first.shape[0] // 2
    row = lax.broadcasted_iota(jnp.int32, (half, half), 0)
    col = lax.broadcasted_iota(jnp.int32, (half, half), 1)
    upper = row <= col

    def mixed(at):
        cut = slice(at, at + half)
        return jnp.where(upper, first[cut, cut], second[cut, cut])

    top = jnp.concatenate([mixed(0), first[:half, half:]], axis=1)
    bottom = jnp.concatenate([second[half:, :half], mixed(half)], axis=1)
    return jnp.concatenate([top, bottom], axis=0).astype(BF16)


def unpack(packed, diagonal, valid):
    half = packed.shape[0] // 2
    packed = jnp.where(valid, packed, jnp.zeros_like(packed))
    diagonal = jnp.where(valid, diagonal.astype(F32), 0.0)
    turned = packed.T
    row = lax.broadcasted_iota(jnp.int32, (half, half), 0)
    col = lax.broadcasted_iota(jnp.int32, (half, half), 1)

    def corners(at):
        cut = slice(at, at + half)
        straight, mirrored = packed[cut, cut].astype(F32), turned[cut, cut].astype(F32)
        low = jnp.where(row <= col, straight, mirrored)
        high = jnp.where(row == col, diagonal[:, cut], jnp.where(row < col, mirrored, straight))
        return low.astype(BF16), high.astype(BF16)

    def whole(north, ne, sw, south):
        top = jnp.concatenate([north, ne], axis=1)
        bottom = jnp.concatenate([sw, south], axis=1)
        return jnp.concatenate([top, bottom], axis=0)

    north, south = corners(0), corners(half)
    first = whole(north[0], packed[:half, half:], turned[half:, :half], south[0])
    second = whole(north[1], turned[:half, half:], packed[half:, :half], south[1])
    return first, second


def advance(env, slots, blocks, weight=None):
    size = blocks[0].shape[-1]
    middles = []
    for state in range(2):
        turned = blocks[state].T
        halves = []
        for insert in range(2):
            part = dot(turned, env[slots[state], insert * size : (insert + 1) * size])
            if weight is not None:
                part = part * weight[insert][state]
            halves.append(part.astype(BF16))
        middles.append(jnp.concatenate(halves, axis=0))
    both = dot(jnp.concatenate(middles, axis=1), jnp.concatenate(blocks, axis=0))
    return both[:size], both[size:]


def one_state(place, env, site, state, tensors, b):
    size = env.shape[-1]
    block = tensors[state, place.local(b)]
    slot = REACH + b + place.steps[2 * site + state]
    turned = block.T
    halves = [dot(turned, env[slot, k * size : (k + 1) * size]).astype(BF16) for k in range(2)]
    return dot(jnp.concatenate(halves, axis=0), block)


def early_state(place, site, b, known):
    nearer = 1 - place.core
    return jnp.where(b + place.steps[2 * site + nearer] < known, nearer, 1 - nearer)


def begin(place, todo, known, env, site, tensors, partial):
    for i, b in enumerate(range(*todo)):
        partial[i] = one_state(place, env, site, early_state(place, site, b, known), tensors, b)


def complete(place, i, b, known, env, site, tensors, partial):
    both = partial[i] + one_state(place, env, site, 1 - early_state(place, site, b, known), tensors, b)
    size = env.shape[-1]
    return both[:size], both[size:]


def squares(place, blocks, weight, b):
    terms = [dot(blocks[state].T, blocks[state]) for state in range(2)]
    out = []
    for insert in range(2):
        total = 0.0
        for state in range(2):
            inside = b + place.steps[state] < place.width
            total = total + jnp.where(inside, weight[insert][state], 0.0) * terms[state]
        out.append(total)
    return out


def fill_steps(place, sources, steps):
    middle = sources.shape[2] // 2
    for site in range(2):
        charge = sources[2 * place.pair + site, 0, middle] - middle + 1
        for state in range(2):
            steps[2 * site + state] = (2 * place.core - 1) * (charge + 2 * state - 1)


def fill_weights(operators, insert_at, weights):
    for which in range(2):
        for k in range(2):
            for s in range(2):
                weights[which, 2 * k + s] = jnp.where(insert_at[0, k] == which, operators[k, s], 1.0)


def weights_at(weights, which):
    return [[weights[which, 2 * k + s] for s in range(2)] for k in range(2)]


def add_traces(place, traces, at, site, b, parts, radius):
    row = radius[place.local(b), pl.ds(2 * place.pair + site, 1)]
    for k in range(2):
        traces[at + k : at + k + 1] += diagonal_row(parts[k].astype(BF16).astype(F32)) * (row * row)


def slots_of(place, site, b):
    return [REACH + b + place.steps[2 * site + state] for state in range(2)]


def store_env(env, slot, parts):
    size = parts[0].shape[0]
    for k in range(2):
        env[slot, k * size : (k + 1) * size] = parts[k].astype(BF16)


def blocks_of(place, tensors, b):
    return [tensors[state, place.local(b)] for state in range(2)]


def send(place, env, t1, weight, traces, radius, sent, run):
    rows = []
    for b in range(*run):
        parts = advance(env, slots_of(place, 1, b), blocks_of(place, t1, b), weight)
        size = parts[0].shape[0]
        sent[(b - run[0]) * size : (b - run[0] + 1) * size] = pack(*parts)
        add_traces(place, traces, 4, 1, b, parts, radius)
        rows.append(diagonal_row(parts[1]))
    return rows


def send_rows(sent, rows):
    rows = jnp.concatenate(rows, axis=0)
    rows = jnp.concatenate([rows, jnp.zeros((EXTRA - rows.shape[0], rows.shape[1]), F32)], axis=0)
    sent[sent.shape[0] - EXTRA :] = rows.astype(BF16)


def below(buffer):
    return buffer[buffer.shape[0] - EXTRA :]


def take(place, buffer, i, diagonals, row, env, slot):
    size = buffer.shape[1]
    store_env(env, slot, unpack(buffer[i * size : (i + 1) * size], diagonals[row : row + 1], place.pair > 0))


class Loads:
    def __init__(self):
        self.waiting = {}

    def start(self, key, source, target, sem):
        copy = pltpu.make_async_copy(source, target, sem)
        copy.start()
        self.waiting[key] = copy

    def tensors(self, place, source, target, site, lo, hi, sem):
        at = pl.ds(jnp.where(place.core == 0, place.width - hi, lo), hi - lo)
        for state in range(2):
            self.start((site, lo, state), source.at[site, state, at], target.at[state, at], sem.at[state])

    def wait(self, *keys):
        for key in keys:
            if key in self.waiting:
                self.waiting.pop(key).wait()


def first_kernel(width, run, sources, operators, insert_at, tensors, schmidt,
                 sent, edge, env, t0, t1, radius, traces, rows, steps, weights, sources_here, operators_here, inserts_here, sems):
    place = Place(width, steps)
    lo, hi = run
    loads = Loads()
    loads.start("sources", sources, sources_here, sems.at[0])
    loads.start("operators", operators, operators_here, sems.at[1])
    loads.start("insert_at", insert_at, inserts_here, sems.at[2])
    near = hi + HALO
    loads.tensors(place, tensors, t0, 0, 0, near, sems.at[pl.ds(3, 2)])
    loads.tensors(place, tensors, t1, 1, lo, hi, sems.at[pl.ds(5, 2)])
    loads.start("radius", schmidt, radius, sems.at[7])
    traces[...] = jnp.zeros_like(traces)
    env[REACH + width :] = jnp.zeros_like(env[REACH + width :])
    loads.wait("sources", "operators", "insert_at")
    fill_steps(place, sources_here, steps)
    fill_weights(operators_here, inserts_here, weights)
    u, v = weights_at(weights, 0), weights_at(weights, 1)
    loads.wait((0, 0, 0), (0, 0, 1))
    for b in range(near):
        blocks = blocks_of(place, t0, b)
        parts = squares(place, blocks, u, b)
        store_env(env, REACH + b, parts)
        if b < HALO:
            store_env(edge, HALO - 1 - b, parts)
            edge[2 * HALO - 1 - b] = jnp.concatenate(blocks, axis=0)
    loads.wait((1, lo, 0), (1, lo, 1), "radius")
    send_rows(rows, send(place, env, t1, v, traces, radius, sent, run))


def second_kernel(width, first_run, runs, steps, weights, tensors, old_env, halo, old_t0, old_t1, radius,
                  old_traces, first_rows, *rest):
    env, t0, t1, sents, (traces, sems) = *rest[:3], rest[3:-2], rest[-2:]
    place = Place(width, steps)
    size = t0.shape[-1]
    lo, hi = first_run
    known = hi + HALO
    loads = Loads()
    loads.tensors(place, tensors, t0, 0, known, width, sems.at[pl.ds(0, 2)])
    loads.tensors(place, tensors, t1, 1, hi, width, sems.at[pl.ds(2, 2)])
    loads.tensors(place, tensors, t1, 1, 0, lo, sems.at[pl.ds(4, 2)])
    u, v = weights_at(weights, 0), weights_at(weights, 1)
    traces[...] = old_traces[...]
    for i in range(HALO):
        env[REACH - HALO + i] = halo[i]
    for b in range(known):
        parts = [env[REACH + b, k * size : (k + 1) * size] for k in range(2)]
        add_traces(place, traces, 0, 0, b, parts, radius)
    loads.wait((0, known, 0), (0, known, 1))
    for b in range(known, width):
        parts = squares(place, blocks_of(place, t0, b), u, b)
        store_env(env, REACH + b, parts)
        add_traces(place, traces, 0, 0, b, parts, radius)
    loads.wait((1, hi, 0), (1, hi, 1), (1, 0, 0), (1, 0, 1))
    rows = []
    for run, sent in zip(runs, sents):
        rows += send(place, env, t1, v, traces, radius, sent, run)
    send_rows(sents[0], rows + [first_rows[: hi - lo].astype(F32)])


def middle_blocks(place, todo, env, middle, t0, traces, radius, partial=None, known=0):
    for i, b in enumerate(range(*todo)):
        if partial is not None and i < partial.shape[0]:
            parts = complete(place, i, b, known, env, 0, t0, partial)
        else:
            parts = advance(env, slots_of(place, 0, b), blocks_of(place, t0, b))
        store_env(middle, REACH + b, parts)
        add_traces(place, traces, 2, 0, b, parts, radius)


def open_kernel(steps, first, env, middle, piece, width):
    for array in (env, middle):
        array[REACH + width :] = jnp.zeros_like(array[REACH + width :])
    piece[...] = first[: piece.shape[0]]


def final_blocks(place, todo, middle, t1, traces, radius, stage, out, sems, partial=None, known=0):
    stores = Loads()
    for i, b in enumerate(range(*todo)):
        if partial is not None and i < partial.shape[0]:
            parts = complete(place, i, b, known, middle, 1, t1, partial)
        else:
            parts = advance(middle, slots_of(place, 1, b), blocks_of(place, t1, b))
        for k in range(2):
            if out is None:
                stage[k, place.local(b)] = parts[k].astype(BF16)
            else:
                stage[b, k] = parts[k].astype(BF16)
        if out is not None:
            stores.start(b, stage.at[b], out.at[0, :, place.local(b)], sems.at[b])
        add_traces(place, traces, 6, 1, b, parts, radius)
    return stores


def edge_kernel(width, run, steps, t0, t1, halo, radius, old_traces, old_env, old_middle, first, ours, near, far,
                out, env, middle, traces, partial0, partial1, stage, sems):
    place = Place(width, steps)
    lo, known = run
    size = t0.shape[-1]
    traces[...] = old_traces[...]
    for i in range(HALO):
        take(place, ours, i, below(ours), i, env, REACH + i)
        take(place, near, i, below(near), i, env, REACH - 1 - i)
        take(place, far, i, below(near), width - (known - lo) + i, env, REACH - 1 - HALO - i)
    for b in range(lo, known):
        take(place, first, b - lo, below(ours), width - known + b, env, REACH + b)
    for i in range(HALO):
        blocks = [halo[HALO + i, state * size : (state + 1) * size] for state in range(2)]
        store_env(middle, REACH - HALO + i, advance(env, slots_of(place, 0, i - HALO), blocks))
    middle_blocks(place, (0, known - HALO), env, middle, t0, traces, radius)
    last = (0, known - 2 * HALO)
    stores = final_blocks(place, last, middle, t1, traces, radius, stage, out, sems)
    begin(place, (known - HALO, known), known, env, 0, t0, partial0)
    begin(place, (last[1], last[1] + HALO), known - HALO, middle, 1, t1, partial1)
    stores.wait(*range(*last))


def next_kernel(width, run, row, steps, t0, t1, radius, old_traces, ours, buffer, old_partial0, old_partial1, old_env, old_middle,
                *rest):
    lo, hi = run
    if hi == width:
        env, middle, traces, totals, stage = rest
        out = sems = None
    else:
        out, env, middle, traces, *results, stage, sems = rest[1:]
    place = Place(width, steps)
    for b in range(lo, hi):
        take(place, buffer, b - lo, below(ours), row + b - lo, env, REACH + b)
    traces[...] = old_traces[...]
    ends = hi == width
    upto = width if ends else hi - HALO
    middle_blocks(place, (lo - HALO, upto), env, middle, t0, traces, radius, old_partial0, lo)
    last = (lo - 2 * HALO, width if ends else upto - HALO)
    stores = final_blocks(place, last, middle, t1, traces, radius, stage, out, sems, old_partial1, lo - HALO)
    if ends:
        totals[...] = jnp.zeros_like(totals)
        sums = jnp.sum(traces[...], axis=1, keepdims=True)
        for j in range(2):
            for t in range(2):
                at = 4 * j + 2 * t
                totals[j, t : t + 1, :2] = jnp.concatenate([sums[at : at + 1], sums[at + 1 : at + 2]], axis=1)
    else:
        begin(place, (upto, upto + results[0].shape[0]), hi, env, 0, t0, results[0])
        begin(place, (last[1], upto), upto, middle, 1, t1, results[1])
    if out is not None:
        stores.wait(*range(*last))


def store_kernel(width, todo, steps, stage, old_out, out, sems):
    place = Place(width, steps)
    lo, hi = todo
    at = pl.ds(jnp.where(place.core == 0, width - hi, lo), hi - lo)
    stores = Loads()
    for k in range(2):
        stores.start(k, stage.at[k, at], out.at[0, k, at], sems.at[k])
    stores.wait(0, 1)


SMEM = pl.BlockSpec(memory_space=pltpu.SMEM)
VMEM = pl.BlockSpec(memory_space=pltpu.VMEM)
HBM = pl.BlockSpec(memory_space=pl.ANY)
PARAMS = pltpu.CompilerParams(vmem_limit_bytes=28 * 2**20)
RUNS = ((2, 5), (0, 2), (5, 8), (8, 10))


def call(kernel, name, scalars, arrays, outs, scratch=(), aliases=None):
    specs = {pltpu.VMEM: VMEM, pltpu.SMEM: SMEM, pltpu.HBM: HBM}
    where = [pltpu.SMEM] * len(scalars) + [pltpu.VMEM if near else pltpu.HBM for _, near in arrays]
    values = [*scalars, *[a for a, _ in arrays]]
    return pl.pallas_call(
        kernel,
        out_shape=tuple(memory(s, d) for s, d, memory in outs),
        in_specs=[specs[w] for w in where],
        out_specs=tuple(specs[memory] for _, _, memory in outs),
        scratch_shapes=list(scratch),
        compiler_params=PARAMS,
        input_output_aliases={} if aliases is None else aliases,
        name=name,
    )(*[pltpu.with_memory_space_constraint(a, w) for a, w in zip(values, where)])


def shards(tensors, sources, operators, insert_at, schmidt):
    width, size = tensors.shape[2], tensors.shape[-1]
    pairs = lax.axis_size("site")
    ring = [(i, (i + 1) % pairs) for i in range(pairs)]
    swap = [(0, 1), (1, 0)]
    schmidt = jnp.swapaxes(schmidt, 0, 1)

    def message(run, extra=EXTRA):
        return ((run[1] - run[0]) * size + extra, size), BF16, pltpu.VMEM

    trace_shape = ((8, size), F32, pltpu.VMEM)
    env_shape = ((width + REACH + HALO, 2 * size, size), BF16, pltpu.VMEM)
    tensor_shape = ((2, width, size, size), BF16, pltpu.VMEM)
    partial_shape = ((HALO, 2 * size, size), F32, pltpu.VMEM)
    radius_shape = (schmidt.shape, F32, pltpu.VMEM)
    out_shape = ((1, 2, width, size, size), BF16, pltpu.HBM)
    stage = [pltpu.VMEM((width, 2, size, size), BF16), pltpu.SemaphoreType.DMA((width,))]

    def across(array):
        return lax.ppermute(array, "sec", swap)

    sent, edge, env, t0, t1, radius, traces, rows, steps, weights = call(
        functools.partial(first_kernel, width, RUNS[0]),
        "anchor",
        (),
        tuple((a, False) for a in (sources, operators, insert_at, tensors, schmidt)),
        (
            message(RUNS[0], 0),
            ((2 * HALO, 2 * size, size), BF16, pltpu.VMEM),
            env_shape,
            tensor_shape,
            tensor_shape,
            radius_shape,
            trace_shape,
            ((EXTRA, size), BF16, pltpu.VMEM),
            ((4,), jnp.int32, pltpu.SMEM),
            ((2, 4), F32, pltpu.SMEM),
        ),
        [pltpu.SMEM(a.shape, a.dtype) for a in (sources, operators, insert_at)] + [pltpu.SemaphoreType.DMA((8,))],
    )
    halo = across(edge)
    got = [lax.ppermute(sent, "site", ring)]
    env, t0, t1, *sents, traces = call(
        functools.partial(second_kernel, width, RUNS[0], RUNS[1:]),
        "anchor_rest",
        (steps, weights),
        ((tensors, False),) + tuple((a, True) for a in (env, halo, t0, t1, radius, traces, rows)),
        (env_shape, tensor_shape, tensor_shape) + (message(RUNS[1]), message(RUNS[2], 0), message(RUNS[3], 0)) + (trace_shape,),
        [pltpu.SemaphoreType.DMA((6,))],
        {3: 0, 5: 1, 6: 2},
    )
    got += [lax.ppermute(s, "site", ring[:-1]) for s in sents]
    env, middle, piece = call(
        functools.partial(open_kernel, width=width),
        "first_run",
        (steps,),
        ((got[0], True),),
        (env_shape, env_shape, message(RUNS[1], 0)),
    )
    ours, env = lax.optimization_barrier((got[1], env))
    final, env, middle, traces, *partials = call(
        functools.partial(edge_kernel, width, RUNS[0]),
        "edge",
        (steps,),
        tuple((a, True) for a in (t0, t1, halo, radius, traces, env, middle, got[0], ours, across(ours), across(piece))),
        (out_shape, env_shape, env_shape, trace_shape, partial_shape, partial_shape),
        stage,
        {6: 1, 7: 2},
    )
    row = RUNS[1][1] - RUNS[1][0]
    run, last = RUNS[2:]
    final, env, middle, traces, *partials = call(
        functools.partial(next_kernel, width, run, row),
        "third_run",
        (steps,),
        tuple((a, True) for a in (t0, t1, radius, traces, ours, got[2], *partials, env, middle)) + ((final, False),),
        (out_shape, env_shape, env_shape, trace_shape, ((2 * HALO, 2 * size, size), F32, pltpu.VMEM), partial_shape),
        stage,
        {9: 1, 10: 2, 11: 0},
    )
    env, middle, traces, totals, blocks = call(
        functools.partial(next_kernel, width, last, row + run[1] - run[0]),
        "last_run",
        (steps,),
        tuple((a, True) for a in (t0, t1, radius, traces, ours, got[3], *partials, env, middle)),
        (env_shape, env_shape, trace_shape, ((2, 16, 128), F32, pltpu.VMEM), ((2, width, size, size), BF16, pltpu.VMEM)),
        aliases={9: 0, 10: 1},
    )
    others = across(totals)
    (final,) = call(
        functools.partial(store_kernel, width, (last[0] - 2 * HALO, width)),
        "store",
        (steps,),
        ((blocks, True), (final, False)),
        (out_shape,),
        stage[1:],
        {2: 0},
    )
    return final, totals[:, :2, :2] + others[:, :2, :2]


def solution(mesh):
    placed = (
        P(("grp", "site"), None, "sec", None, None),
        P("grp", None, None),
        P(),
        P(("grp", "site"), None),
        P("grp", "sec", None),
    )
    return jax.shard_map(
        shards,
        mesh=mesh,
        in_specs=placed,
        out_specs=(P(("grp", "site"), None, "sec", None, None), P(("grp", "site"), None, None)),
        check_vma=False,
    )
```
